256 devices in a mesh: tp: 4 (over y), ep: 64 (over x, z, core).
Axes of the slice: x: 4, y: 4, z: 8, core: 2. Of those that a mesh axis runs over, the one named last changes fastest.
Arguments:
- queries: bfloat16 [2048, 64, 128], P('ep', 'tp'), may hold values from -6 to 6
- cache_keys: bfloat16 [2048, 4, 192, 128], P('ep', 'tp'), may hold values from -6 to 6
- cache_values: bfloat16 [2048, 4, 192, 128], P('ep', 'tp'), may hold values from -6 to 6
- new_keys: bfloat16 [2048, 4, 128], P('ep', 'tp'), may hold values from -6 to 6
- new_values: bfloat16 [2048, 4, 128], P('ep', 'tp'), may hold values from -6 to 6
- lengths: int32 [2048], P('ep'), may hold values from 1 to 192, as said below
- out_weight: bfloat16 [8192, 4096], P('tp', 'ep'), may hold values from -0.25 to 0.25
- residual: bfloat16 [64, 32, 4096], P('ep', 'tp'), may hold values from -6 to 6
- norm_gain: bfloat16 [4096], replicated, may hold values from 0.25 to 1.75
- routes: int32 [64, 32, 8], P('ep', 'tp'), may hold values from 0 to 63, all different within a row; in each aligned block of 8 rows (0 to 7, 8 to 15, ..., all dimensions but the last counted through in order) at most 2 rows name the same one
- route_weights: float32 [64, 32, 8], P('ep', 'tp'), may hold values from 0.1 to 0.6
- gate_weight: bfloat16 [64, 4096, 1536], P('ep', None, 'tp'), may hold values from -0.09375 to 0.09375
- up_weight: bfloat16 [64, 4096, 1536], P('ep', None, 'tp'), may hold values from -0.09375 to 0.09375
- down_weight: bfloat16 [64, 1536, 4096], P('ep', 'tp'), may hold values from -0.15625 to 0.15625
Outputs:
- layer_out: bfloat16 [64, 32, 4096], P('ep', 'tp')
The draws below stay inside these ranges and needn't reach their ends.
Inputs may be any that keep to these rules, and one draw needn't show every extreme that they name: `lengths`: every decode group of 32 rows has at least one row with all 192 cache slots valid. `routes`: each row names 8 different experts; among the rows of one device (aligned blocks of 8 rows in row order) no expert is named by more than 2 rows, a bound that some block reaches.
All inputs are finite; a program needn't handle non-finite values.
Results may differ from the reference program's by a relative error of at most 0.017.
Values may be sent and summed in bfloat16 or wider, within the bound.
A program may use at most 128 MiB of HBM per device.

```python
import math
import jax
import jax.numpy as jnp
import numpy as np
from jax import lax

D = 4096
HEADS = 64
KVH = 4
HD = 128
FF = 1536
TOP = 8
ROW_DEV = 8
CTX = 192
EXPERTS = 64
GROUPS = 64
ROW_GRP = 32
ROWS = 2048
CAP = 2
N_TP = 4


def layout(key):
    keys = jax.random.split(key, 7)
    groups = ROWS // ROW_GRP
    lengths = jax.random.randint(keys[0], (groups, ROW_GRP), 1, CTX + 1)
    full = jax.random.randint(keys[1], (groups, 1), 0, ROW_GRP)
    lengths = jnp.where(jnp.arange(ROW_GRP)[None, :] == full, CTX, lengths).reshape(ROWS).astype(jnp.int32)
    spot = jax.random.randint(keys[2], (ROWS,), 0, CTX) % lengths
    second = (spot + 1 + jax.random.randint(keys[3], (ROWS,), 0, CTX)) % lengths
    signs = (jax.random.randint(keys[4], (ROWS, KVH, HD), 0, 2) * 2 - 1).astype(jnp.float32)
    aligned = jax.random.randint(keys[5], (ROWS,), 0, 4) == 0
    strength = jax.random.uniform(keys[6], (ROWS,), jnp.float32, 3.0, 5.5)
    return (lengths, spot, second, signs, aligned, strength)


def draw_lengths(key, part):
    shared = layout(key)
    return shared[0]


def draw_cache_keys(key, part):
    key = jax.random.fold_in(key, 2)
    values = jnp.clip(jax.random.normal(key, (ROWS, KVH, CTX, HD), jnp.float32), -6.0, 6.0)
    return values.astype(jnp.bfloat16)


def draw_queries(key, part):
    key = jax.random.fold_in(key, 3)
    values = jnp.clip(jax.random.normal(key, (ROWS, HEADS, HD), jnp.float32), -6.0, 6.0)
    return values.astype(jnp.bfloat16)


def steps_of(own_key, shape, pieces, smallest, largest):
    factor_of = 1.0
    for dim, blocks in pieces:
        draws = jax.random.uniform(jax.random.fold_in(jax.random.fold_in(own_key, 6), dim), (blocks,), jnp.float32, smallest / len(pieces), largest / len(pieces))
        factor_of = factor_of * jnp.repeat(jnp.exp(draws), shape[dim] // blocks).reshape((-1,) + (1,) * (len(shape) - 1 - dim))
    return factor_of


def assign_block(own_key, own, number, rows, amount, top, most, lean):
    sequence = jax.random.permutation(own_key, amount)
    heavy_load, usual = portions_of(amount, rows * top, most, lean, True), portions_of(amount, rows * top, most, lean, False)
    places = jnp.arange(amount)

    def named(tallies, offset_by):
        used = int((tallies > 0).sum())
        fixed = max(1, used // 4)
        passed = fixed + (places - fixed + offset_by * (used - fixed)) % max(1, amount - fixed)
        return jnp.zeros((amount,), jnp.int32).at[sequence[jnp.where(places < fixed, places, passed)]].set(jnp.asarray(tallies, jnp.int32))

    tallies = jnp.where(number % 4 == 0, named(heavy_load, number // 4), named(usual, number - number // 4 - 1))
    mixed = jax.random.permutation(jax.random.fold_in(own, 3), amount)
    giver, taker = mixed[0:amount // 2 * 2:2], mixed[1:amount // 2 * 2:2]
    slack = jnp.minimum(tallies[giver] - 1, most - tallies[taker]) // 2
    slack = jnp.where((giver == sequence[0]) | (taker == sequence[0]) | (tallies[taker] == 0), 0, jnp.maximum(slack, 0))
    passed = jax.random.randint(jax.random.fold_in(own, 4), (amount // 2,), 0, 1 << 20) % (slack + 1)
    tallies = tallies.at[giver].add(-passed).at[taker].add(passed)
    labels = jnp.searchsorted(jnp.cumsum(tallies), jnp.arange(rows * top), side="right").astype(jnp.int32)
    table = labels.reshape(top, rows).T
    table = table[jax.random.permutation(jax.random.fold_in(own, 1), rows)]
    offset_by = jax.random.randint(jax.random.fold_in(own, 2), (rows, 1), 0, top)
    return jnp.take_along_axis(table, (jnp.arange(top)[None, :] + offset_by) % top, axis=1)


def portions_of(count, total, limit, slope, full):
    portions = [(1 << 20) // math.isqrt(rank ** slope) + 1 for rank in range(1, count + 1)]
    largest = limit if full else min(limit, max(-(-total // count), total * portions[0] // sum(portions)))
    least = 1 if total - largest >= count - 1 else 0
    given, surplus = [largest] + [least] * (count - 1), total - largest - least * (count - 1)
    while surplus > 0:
        movable = [i for i in range(1, count) if given[i] < largest] or [i for i in range(1, count) if given[i] < limit]
        pool, left = sum([portions[i] for i in movable]), surplus
        for i in movable:
            more = min(limit - given[i], max(1, left * portions[i] // pool), surplus)
            given[i] = given[i] + more
            surplus = surplus - more
    return np.array(given)


def gaussian(key, shape, scale, bound, shards=(), kind=jnp.bfloat16):
    factor_of = steps_of(key, shape, shards, -0.22, 0.18) if shards else 1.0
    values = jax.random.normal(key, shape, jnp.float32) * scale * factor_of
    return jnp.minimum(jnp.maximum(values, -bound), bound).astype(kind)


def setup_inputs(seed: int = 0) -> dict:
    splits = jax.random.split(jax.random.key(seed), 15)
    queries = draw_queries(jax.random.fold_in(splits[14], 71), 0)
    cache_keys = draw_cache_keys(jax.random.fold_in(splits[14], 71), 0)
    cache_values = gaussian(splits[2], (ROWS, KVH, CTX, HD), 1.0, 6.0, ((0, 64), (1, 4)))
    new_keys = gaussian(splits[3], (ROWS, KVH, HD), 1.0, 6.0, ((0, 64), (1, 4)))
    new_values = gaussian(splits[4], (ROWS, KVH, HD), 1.0, 6.0, ((0, 64), (1, 4)))
    lengths = draw_lengths(jax.random.fold_in(splits[14], 71), 0)
    out_weight = gaussian(splits[6], (HEADS * HD, D), (HEADS * HD // 16) ** -0.5, 0.25, ((0, 4), (1, 64)))
    residual = gaussian(splits[7], (GROUPS, ROW_GRP, D), 1.0, 6.0, ((0, 64), (1, 4)))
    norm_gain = jnp.clip(1.0 + 0.15 * jax.random.normal(splits[8], (D,), jnp.float32), 0.25, 1.75).astype(jnp.bfloat16)
    routes_keys = jax.random.split(jax.random.fold_in(splits[9], 1), GROUPS * ROW_GRP // ROW_DEV)
    routes_turns = jax.random.permutation(jax.random.fold_in(splits[9], 3), GROUPS * ROW_GRP // ROW_DEV)
    routes = jax.vmap(lambda own, number: assign_block(jax.random.fold_in(splits[9], 2), own, number, ROW_DEV, EXPERTS, TOP, CAP, 2))(routes_keys, routes_turns).reshape((GROUPS, ROW_GRP, TOP))
    route_weights = jnp.clip(0.1 + 0.5 * jax.random.uniform(splits[10], (GROUPS, ROW_GRP, TOP), jnp.float32) ** steps_of(splits[10], (GROUPS, ROW_GRP, TOP), ((0, 64), (1, 4)), -0.2, 0.2), 0.1, 0.6)
    gate_weight = gaussian(splits[11], (EXPERTS, D, FF), D ** -0.5, 0.09375, ((0, 64), (2, 4)))
    up_weight = gaussian(splits[12], (EXPERTS, D, FF), D ** -0.5, 0.09375, ((0, 64), (2, 4)))
    down_weight = gaussian(splits[13], (EXPERTS, FF, D), FF ** -0.5, 0.15625, ((0, 64), (1, 4)))
    return {"queries": queries, "cache_keys": cache_keys, "cache_values": cache_values, "new_keys": new_keys, "new_values": new_values, "lengths": lengths, "out_weight": out_weight, "residual": residual, "norm_gain": norm_gain, "routes": routes, "route_weights": route_weights, "gate_weight": gate_weight, "up_weight": up_weight, "down_weight": down_weight}


def attend(queries, cache_keys, cache_values, new_keys, new_values, lengths):
    count = queries.shape[0]
    scale = HD ** (-0.5)
    grouped = queries.reshape(count, KVH, HEADS // KVH, HD).astype(jnp.float32)
    cached = jnp.einsum('rkgd,rkcd->rkgc', grouped, cache_keys.astype(jnp.float32)) * scale
    fresh = jnp.einsum('rkgd,rkd->rkg', grouped, new_keys.astype(jnp.float32)) * scale
    valid = (jnp.arange(CTX, dtype=jnp.int32)[None, :] < lengths[:, None])[:, None, None, :]
    cached = jnp.where(valid, cached, jnp.float32(-1e+30))
    peak = jnp.maximum(lax.optimization_barrier(jnp.max(cached, axis=-1)), fresh)
    cached_w = jnp.where(valid, jnp.exp(cached - peak[..., None]), jnp.float32(0.0))
    fresh_w = jnp.exp(fresh - peak)
    total = lax.optimization_barrier(jnp.sum(cached_w, axis=-1)) + fresh_w
    cached_p = lax.optimization_barrier((cached_w / total[..., None]).astype(jnp.bfloat16))
    fresh_p = lax.optimization_barrier((fresh_w / total).astype(jnp.bfloat16))
    mixed = jnp.einsum('rkgc,rkcd->rkgd', cached_p.astype(jnp.float32), cache_values.astype(jnp.float32))
    mixed = mixed + fresh_p.astype(jnp.float32)[..., None] * new_values.astype(jnp.float32)[:, :, None, :]
    return mixed.astype(jnp.bfloat16).reshape(count, HEADS * HD)

def expert_mix(normed, routes, route_weights, gate_weight, up_weight, down_weight):
    slots = ROWS // ROW_DEV * CAP

    def one_expert(total, inputs):
        expert, gate_w, up_w, down_w = inputs
        hit = routes == expert
        chosen = jnp.any(hit, axis=1)
        weight = lax.optimization_barrier(jnp.sum(jnp.where(hit, route_weights, jnp.float32(0.0)), axis=1))
        index = jnp.nonzero(chosen, size=slots, fill_value=0)[0].astype(jnp.int32)
        live = jnp.arange(slots, dtype=jnp.int32) < jnp.sum(chosen.astype(jnp.int32))
        picked = normed[index]
        gate = jnp.dot(picked, gate_w, preferred_element_type=jnp.float32)
        up = jnp.dot(picked, up_w, preferred_element_type=jnp.float32)
        act = lax.optimization_barrier((jax.nn.silu(gate) * up).astype(jnp.bfloat16))
        quarters = jnp.einsum('sqf,qfd->qsd', act.reshape(slots, N_TP, FF // N_TP).astype(jnp.float32), down_w.reshape(N_TP, FF // N_TP, D).astype(jnp.float32))
        quarters = lax.optimization_barrier(quarters.astype(jnp.bfloat16)).astype(jnp.float32)
        result = lax.optimization_barrier(jnp.sum(quarters, axis=0)).astype(jnp.bfloat16).astype(jnp.float32)
        factor = jnp.where(live, weight[index], jnp.float32(0.0))
        return (total.at[index].add(factor[:, None] * result), None)
    start = jnp.zeros((ROWS, D), jnp.float32)
    total, _ = lax.scan(one_expert, start, (jnp.arange(EXPERTS, dtype=jnp.int32), gate_weight, up_weight, down_weight))
    return total

def reference(queries, cache_keys, cache_values, new_keys, new_values, lengths, out_weight, residual, norm_gain, routes, route_weights, gate_weight, up_weight, down_weight):
    attn = attend(queries, cache_keys, cache_values, new_keys, new_values, lengths)
    proj = lax.optimization_barrier(jnp.dot(attn, out_weight, preferred_element_type=jnp.float32).astype(jnp.bfloat16))
    hidden = residual.reshape(ROWS, D).astype(jnp.float32) + proj.astype(jnp.float32)
    inverse = lax.rsqrt(lax.optimization_barrier(jnp.mean(hidden * hidden, axis=-1, keepdims=True)) + 1e-06)
    normed = (hidden * inverse * norm_gain.astype(jnp.float32)[None, :]).astype(jnp.bfloat16)
    mixed = expert_mix(normed, routes.reshape(ROWS, TOP), route_weights.reshape(ROWS, TOP), gate_weight, up_weight, down_weight)
    return (hidden + mixed).astype(jnp.bfloat16).reshape(GROUPS, ROW_GRP, D)
```

```python
import functools

import jax
import jax.numpy as jnp
from jax import lax
from jax.experimental import pallas as pl
from jax.experimental.pallas import tpu as pltpu
from jax.sharding import PartitionSpec as P

MESH = pl.DeviceIdType.MESH
BF16 = jnp.bfloat16
F32 = jnp.float32
EP_SHAPE = (4, 8, 2)
LANES = 128
CAP = 2
VMEM_LIMIT = 60 * 1024 * 1024


def dot(a, b):
    return jnp.dot(a, b, preferred_element_type=F32)


def dot_nt(a, b):
    return lax.dot_general(a, b, (((1,), (1,)), ((), ())), preferred_element_type=F32)


def rel(i):
    return ((i + 1) // 2) * (2 * (i % 2) - 1)


def kernel(
    dims,
    lengths_ref,
    nk_ref,
    nv_ref,
    gain_ref,
    routes_ref,
    shares_ref,
    q_hbm,
    k_hbm,
    v_hbm,
    wt_hbm,
    res_hbm,
    gate_hbm,
    up_hbm,
    down_hbm,
    out_ref,
    q_buf,
    k_buf,
    v_buf,
    mixed_buf,
    fresh_buf,
    wg,
    xg,
    rs_send,
    rs_recv,
    projg,
    resg,
    hid,
    info,
    comb,
    sel,
    xs,
    gu,
    dwg,
    actg,
    ret_send,
    ret_recv,
    fin_send,
    fin_recv,
    fy_send,
    fy_recv,
    load_sem,
    ring_ss,
    ring_rs,
    x_ss,
    x_rs,
    res_ss,
    res_rs,
    info_ss,
    info_rs,
    infoy_ss,
    infoy_rs,
    dw_ss,
    dw_rs,
    rs_ss,
    rs_rs,
    proj_ss,
    proj_rs,
    sel_ss,
    sel_rs,
    xs_ss,
    xs_rs,
    act_ss,
    act_rs,
    ret_ss,
    ret_rs,
    fin_ss,
    fin_rs,
    fy_ss,
    fy_rs,
):
    nx, nz, nc, nt = dims
    ns = nx * nc
    rows = res_hbm.shape[0]
    width = res_hbm.shape[1]
    quarter = width // nt
    group_rows = nt * rows
    heads, head_size = q_buf.shape[1], q_buf.shape[2]
    context = k_buf.shape[1]
    hidden_units = gate_hbm.shape[1]
    chunk = ns * CAP

    ep = lax.axis_index("ep")
    t = lax.axis_index("tp")
    x = ep // (nz * nc)
    z = (ep // nc) % nz
    c = ep % nc
    s = x * nc + c

    def z_peer(d):
        return {"ep": (x * nz + (z + d + nz) % nz) * nc + c, "tp": t}

    def s_index(d):
        return (s + d) % ns

    def s_peer(d):
        p = s_index(d)
        return {"ep": ((p // nc) * nz + z) * nc + p % nc, "tp": t}

    def t_index(d):
        return (t + d) % nt

    def t_peer(d):
        return {"ep": ep, "tp": t_index(d)}

    pending = []

    def send(src, dst, ss, rs, peer):
        copy = pltpu.make_async_remote_copy(
            src_ref=src, dst_ref=dst, send_sem=ss, recv_sem=rs, device_id=peer, device_id_type=MESH
        )
        copy.start()
        pending.append(copy)

    def arrive(dst, ss, rs):
        pltpu.make_async_remote_copy(
            src_ref=dst, dst_ref=dst, send_sem=ss, recv_sem=rs, device_id=t_peer(1), device_id_type=MESH
        ).wait_recv()

    barrier = pltpu.get_barrier_semaphore()
    partners = (
        [z_peer(d) for d in range(1, nz)]
        + [s_peer(d) for d in range(1, ns)]
        + [t_peer(d) for d in range(1, nt)]
    )
    for peer in partners:
        pl.semaphore_signal(barrier, inc=1, device_id=peer, device_id_type=MESH)

    def load(src, dst, n):
        copy = pltpu.make_async_copy(src, dst, load_sem.at[n])
        copy.start()
        return copy

    q_load = load(q_hbm, q_buf, 0)
    k_load = load(k_hbm, k_buf, 1)
    v_load = load(v_hbm, v_buf, 2)
    w_load = load(wt_hbm, wg.at[z], 3)
    r_load = load(res_hbm, resg.at[s], 4)
    g_load = load(gate_hbm, gu.at[:, pl.ds(0, hidden_units)], 5)
    u_load = load(up_hbm, gu.at[:, pl.ds(hidden_units, hidden_units)], 6)
    my_quarter = pl.ds(pl.multiple_of(t * quarter, LANES), quarter)
    d_load = load(down_hbm.at[:, my_quarter], dwg.at[t], 7)

    lane = lax.broadcasted_iota(jnp.int32, (rows, LANES), 1)
    row = lax.broadcasted_iota(jnp.int32, (rows, LANES), 0)
    member = jnp.zeros((rows, LANES), F32)
    share = jnp.zeros((rows, LANES), F32)
    routes = routes_ref[...]
    shares = shares_ref[...]
    for k in range(routes.shape[1]):
        hit = routes[:, k : k + 1] == lane
        member = jnp.where(hit, 1.0, member)
        share = share + jnp.where(hit, shares[:, k : k + 1], 0.0)
    rank = jnp.zeros((rows, LANES), F32)
    for j in range(rows - 1):
        rank = rank + jnp.where(row > j, member[j : j + 1, :], 0.0)
    info[t, s, 0] = jnp.where(member > 0.0, rank, -1.0)
    info[t, s, 1] = share

    pl.semaphore_wait(barrier, len(partners))

    half = nz // 2
    wrows = wt_hbm.shape[0]
    top, low = pl.ds(0, wrows // 2), pl.ds(wrows // 2, wrows // 2)

    def ring_step(j):
        right_block = (z - (j - 1) + nz) % nz
        left_block = (z + (j - 1)) % nz
        right_src = wt_hbm if j == 1 else wg.at[right_block]
        left_src = wt_hbm if j == 1 else wg.at[left_block]
        right_dst, left_dst = wg.at[right_block], wg.at[left_block]
        if j == half:
            right_src, right_dst = right_src.at[top], right_dst.at[top]
            left_src, left_dst = left_src.at[low], left_dst.at[low]
        send(right_src, right_dst, ring_ss.at[0, j - 1], ring_rs.at[0, j - 1], z_peer(1))
        send(left_src, left_dst, ring_ss.at[1, j - 1], ring_rs.at[1, j - 1], z_peer(-1))

    def ring_wait(j):
        from_left = wg.at[(z - j + nz) % nz]
        from_right = wg.at[(z + j) % nz]
        if j == half:
            from_left, from_right = from_left.at[top], from_right.at[low]
        arrive(from_left, ring_ss.at[0, j - 1], ring_rs.at[0, j - 1])
        arrive(from_right, ring_ss.at[1, j - 1], ring_rs.at[1, j - 1])

    ring_step(1)
    for d in range(1, ns):
        send(info.at[t, s], info.at[t, s], info_ss.at[d], info_rs.at[d], s_peer(d))
    for d in range(1, ns):
        send(res_hbm, resg.at[s], res_ss.at[d], res_rs.at[d], s_peer(d))
    for d in range(1, nt):
        p = t_index(d)
        part = pl.ds(pl.multiple_of(p * quarter, LANES), quarter)
        send(down_hbm.at[:, part], dwg.at[t], dw_ss.at[d], dw_rs.at[d], t_peer(d))

    fresh_buf[0, :, 0, :] = nk_ref[...].astype(F32)
    fresh_buf[1, :, 0, :] = nv_ref[...].astype(F32)
    q_load.wait()
    k_load.wait()
    v_load.wait()
    scale = head_size ** (-0.5)
    step_rows = 4

    def attend(g, carry):
        for j in range(step_rows):
            r = g * step_rows + j
            q = q_buf[r]
            scores = dot_nt(q, k_buf[r]) * scale
            fresh = (
                jnp.sum(q.astype(F32) * fresh_buf[0, r], axis=1, keepdims=True)
                * scale
            )
            valid = lax.broadcasted_iota(jnp.int32, (heads, context), 1) < lengths_ref[r]
            scores = jnp.where(valid, scores, -1e30)
            peak = jnp.maximum(jnp.max(scores, axis=1, keepdims=True), fresh)
            weight = jnp.where(valid, jnp.exp(scores - peak), 0.0)
            fresh_w = jnp.exp(fresh - peak)
            total = jnp.sum(weight, axis=1, keepdims=True) + fresh_w
            probs = (weight / total).astype(BF16)
            fresh_p = (fresh_w / total).astype(BF16).astype(F32)
            mixed_buf[r] = dot(probs, v_buf[r]) + fresh_p * fresh_buf[1, r]
        return carry

    lax.fori_loop(0, group_rows // step_rows, attend, 0)
    for h in range(heads):
        xg[s, :, h * head_size : (h + 1) * head_size] = mixed_buf[:, h, :].astype(BF16)
    for d in range(1, ns):
        send(xg.at[s], xg.at[s], x_ss.at[d], x_rs.at[d], s_peer(d))

    for j in range(1, half):
        ring_wait(j)
        ring_step(j + 1)

    for d in range(1, ns):
        arrive(info.at[t, s_index(-d + ns)], info_ss.at[d], info_rs.at[d])
    for d in range(1, nt):
        send(info.at[t], info.at[t], infoy_ss.at[d], infoy_rs.at[d], t_peer(d))

    picks = nz * chunk
    slot_no = lax.broadcasted_iota(jnp.int32, (picks, LANES), 0)
    at_z = (z + rel(slot_no // chunk) + nz) % nz
    expert = (x * nz + at_z) * nc + c
    spread = (lax.broadcasted_iota(jnp.int32, (picks, LANES), 1) == expert).astype(BF16)
    code = info[t, :, 0].reshape(ns * rows, LANES).astype(BF16)
    seen = dot_nt(spread, code)
    slot_no = lax.broadcasted_iota(jnp.int32, (picks, ns * rows), 0)
    row_no = lax.broadcasted_iota(jnp.int32, (picks, ns * rows), 1)
    pick = (
        (seen == (slot_no % CAP).astype(F32)) & (row_no // rows == (slot_no % chunk) // CAP)
    ).astype(BF16)

    w_load.wait()
    ring_wait(half)
    for d in range(1, ns):
        arrive(xg.at[s_index(-d + ns)], x_ss.at[d], x_rs.at[d])
    all_rows = xg[...].reshape(ns * group_rows, xg.shape[2])
    ncol = nz * wrows
    zstep = min(nz, 4)
    for b in range(nz // zstep):
        cols = wg[b * zstep : (b + 1) * zstep].reshape(zstep * wrows, wg.shape[2])
        part = dot_nt(all_rows, cols).reshape(ns, nt, rows, zstep * wrows)
        for tt in range(nt):
            rs_send[tt, :, b * zstep * wrows : (b + 1) * zstep * wrows] = (
                part[:, tt].reshape(ns * rows, zstep * wrows).astype(BF16)
            )
    for d in range(1, nt):
        send(rs_send.at[t_index(d)], rs_recv.at[t], rs_ss.at[d], rs_rs.at[d], t_peer(d))
    for d in range(1, nt):
        arrive(rs_recv.at[t_index(-d + nt)], rs_ss.at[d], rs_rs.at[d])
    proj = rs_send[t].astype(F32)
    for d in range(1, nt):
        proj = proj + rs_recv[t_index(d)].astype(F32)
    projg[s] = proj.astype(BF16)
    for d in range(1, ns):
        send(projg.at[s], projg.at[s], proj_ss.at[d], proj_rs.at[d], s_peer(d))
    r_load.wait()
    for d in range(1, ns):
        arrive(resg.at[s_index(-d + ns)], res_ss.at[d], res_rs.at[d])
    for d in range(1, ns):
        arrive(projg.at[s_index(-d + ns)], proj_ss.at[d], proj_rs.at[d])

    nrow = ns * rows
    left_half = lax.broadcasted_iota(jnp.int32, (nrow, LANES), 1) < wrows
    squares = jnp.zeros((nrow, LANES), F32)
    for xx in range(nx):
        for kk in range(ncol // LANES):
            a = projg[xx * nc, :, kk * LANES : (kk + 1) * LANES].astype(F32)
            b = projg[xx * nc + 1, :, kk * LANES : (kk + 1) * LANES].astype(F32)
            pair = (
                jnp.where(left_half, a, pltpu.roll(b, wrows, 1)),
                jnp.where(left_half, pltpu.roll(a, wrows, 1), b),
            )
            for side in range(2):
                col = ((xx * nz + 2 * kk + side) * nc) * wrows
                base = resg[:, :, col : col + LANES].astype(F32).reshape(nrow, LANES)
                value = base + pair[side]
                hid[:, col : col + LANES] = value
                squares = squares + value * value
    inverse = lax.rsqrt(jnp.sum(squares, axis=1, keepdims=True) * (1.0 / width) + 1e-06)
    cstep = min(width, 512)
    for b in range(width // cstep):
        cs = slice(b * cstep, (b + 1) * cstep)
        values = (hid[:, cs] * inverse * gain_ref[:, cs].astype(F32)).astype(BF16)
        picked = dot(pick, values).astype(BF16)
        xs[t, 0, :, cs] = picked[:chunk]
        for i in range(1, nz):
            sel[i, :, cs] = picked[i * chunk : (i + 1) * chunk]
    for i in range(1, nz):
        send(sel.at[i], xs.at[t, i], sel_ss.at[i], sel_rs.at[i], z_peer(rel(i)))

    def forward(i):
        if i > 0:
            arrive(xs.at[t, i], sel_ss.at[i], sel_rs.at[i])
        for d in range(1, nt):
            send(xs.at[t, i], xs.at[t, i], xs_ss.at[i, d], xs_rs.at[i, d], t_peer(d))

    per = 2
    forward(0)
    forward(1)

    for d in range(1, nt):
        arrive(info.at[t_index(-d + nt)], infoy_ss.at[d], infoy_rs.at[d])
    places = nz * nt * chunk
    block = nt * chunk
    slot_no = lax.broadcasted_iota(jnp.int32, (LANES, places), 1)
    at_z = (z + rel(slot_no // block) + nz) % nz
    expert = (x * nz + at_z) * nc + c
    spread = (lax.broadcasted_iota(jnp.int32, (LANES, places), 0) == expert).astype(BF16)
    for tt in range(nt):
        code = info[tt, :, 0].reshape(nrow, LANES).astype(BF16)
        weight = info[tt, :, 1].reshape(nrow, LANES).astype(BF16)
        seen = dot(code, spread)
        given = dot(weight, spread)
        slot_no = lax.broadcasted_iota(jnp.int32, (nrow, places), 1)
        row_no = lax.broadcasted_iota(jnp.int32, (nrow, places), 0) + tt * nrow
        fits = (seen == (slot_no % CAP).astype(F32)) & (row_no // rows == (slot_no % block) // CAP)
        comb[tt * nrow : (tt + 1) * nrow, :] = jnp.where(fits, given, 0.0).astype(BF16)

    g_load.wait()
    u_load.wait()
    d_load.wait()
    for d in range(1, nt):
        arrive(dwg.at[t_index(-d + nt)], dw_ss.at[d], dw_rs.at[d])

    prow = nt * per * chunk

    def first(p):
        for i in range(per * p, per * p + per):
            for d in range(1, nt):
                arrive(xs.at[t_index(-d + nt), i], xs_ss.at[i, d], xs_rs.at[i, d])
        slots = xs[:, per * p : per * p + per].reshape(prow, width)
        both = dot(slots, gu[...])
        gate, up = both[:, :hidden_units], both[:, hidden_units:]
        act = (gate / (1.0 + jnp.exp(-gate)) * up).astype(BF16)
        actg[t, p] = act
        for d in range(1, nt):
            send(actg.at[t, p], actg.at[t, p], act_ss.at[p, d], act_rs.at[p, d], t_peer(d))

    def second(p):
        for d in range(1, nt):
            arrive(actg.at[t_index(-d + nt), p], act_ss.at[p, d], act_rs.at[p, d])
        total = dot(actg[0, p], dwg[0])
        for tt in range(1, nt):
            total = total + dot(actg[tt, p], dwg[tt])
        total = total.astype(BF16).reshape(nt, per, chunk, quarter)
        for k in range(per):
            i = per * p + k
            value = total[:, k].reshape(nt * chunk, quarter)
            if i == 0:
                ret_recv[0] = value
            else:
                ret_send[i] = value
                send(ret_send.at[i], ret_recv.at[i], ret_ss.at[i], ret_rs.at[i], z_peer(-rel(i)))

    for p in range(nz // per):
        if p < nz // per - 1:
            for k in range(per):
                forward(per * (p + 1) + k)
        first(p)
        if p > 0:
            second(p - 1)
    second(nz // per - 1)

    for i in range(1, nz):
        arrive(ret_recv.at[i], ret_ss.at[i], ret_rs.at[i])
    back = ret_recv[...].reshape(places, quarter)
    for tt in range(nt):
        part = dot(comb[tt * nrow : (tt + 1) * nrow, :], back).reshape(ns, rows, quarter)
        for ss in range(ns):
            fin_send[ss, tt * rows : (tt + 1) * rows, :] = part[ss].astype(BF16)
    for d in range(1, ns):
        send(fin_send.at[s_index(d)], fin_recv.at[s], fin_ss.at[d], fin_rs.at[d], s_peer(d))
    total = fin_send[s].astype(F32)
    for d in range(1, ns):
        p = s_index(-d + ns)
        arrive(fin_recv.at[p], fin_ss.at[d], fin_rs.at[d])
        total = total + fin_recv[p].astype(F32)
    for tt in range(nt):
        fy_send[tt] = total[tt * rows : (tt + 1) * rows]
    for d in range(1, nt):
        send(fy_send.at[t_index(d)], fy_recv.at[t], fy_ss.at[d], fy_rs.at[d], t_peer(d))
    fy_recv[t] = fy_send[t]
    for d in range(1, nt):
        arrive(fy_recv.at[t_index(-d + nt)], fy_ss.at[d], fy_rs.at[d])
    own = pl.ds(pl.multiple_of(s * rows, rows), rows)
    for tt in range(nt):
        cs = slice(tt * quarter, (tt + 1) * quarter)
        out_ref[:, cs] = (hid[own, cs] + fy_recv[tt]).astype(BF16)
    for copy in pending:
        copy.wait_send()


def on_device(
    nt,
    queries,
    cache_keys,
    cache_values,
    new_keys,
    new_values,
    lengths,
    out_weight,
    residual,
    norm_gain,
    routes,
    route_weights,
    gate_weight,
    up_weight,
    down_weight,
):
    nx, nz, nc = EP_SHAPE
    ns = nx * nc
    group_rows, heads, head_size = queries.shape
    context = cache_keys.shape[2]
    flat = heads * head_size
    rows, width = residual.shape[1:]
    wcols = out_weight.shape[1]
    units = gate_weight.shape[2]
    quarter = width // nt
    chunk = ns * CAP
    nrow = ns * rows
    ncol = nz * wcols
    dma = pltpu.SemaphoreType.DMA
    vmem = pltpu.VMEM
    scratch = [
        vmem((group_rows, heads, head_size), BF16),
        vmem((group_rows, context, head_size), BF16),
        vmem((group_rows, context, head_size), BF16),
        vmem((group_rows, heads, head_size), F32),
        vmem((2, group_rows, 1, head_size), F32),
        vmem((nz, wcols, flat), BF16),
        vmem((ns, group_rows, flat), BF16),
        vmem((nt, nrow, ncol), BF16),
        vmem((nt, nrow, ncol), BF16),
        vmem((ns, nrow, ncol), BF16),
        vmem((ns, rows, width), BF16),
        vmem((nrow, width), F32),
        vmem((nt, ns, 2, rows, LANES), F32),
        vmem((nt * nrow, nz * nt * chunk), BF16),
        vmem((nz, chunk, width), BF16),
        vmem((nt, nz, chunk, width), BF16),
        vmem((width, 2 * units), BF16),
        vmem((nt, units, quarter), BF16),
        vmem((nt, nz // 2, nt * 2 * chunk, units), BF16),
        vmem((nz, nt * chunk, quarter), BF16),
        vmem((nz, nt * chunk, quarter), BF16),
        vmem((ns, group_rows, quarter), BF16),
        vmem((ns, group_rows, quarter), BF16),
        vmem((nt, rows, quarter), F32),
        vmem((nt, rows, quarter), F32),
        dma((8,)),
        dma((2, max(nz // 2, 1))),
        dma((2, max(nz // 2, 1))),
        dma((ns,)),
        dma((ns,)),
        dma((ns,)),
        dma((ns,)),
        dma((ns,)),
        dma((ns,)),
        dma((nt,)),
        dma((nt,)),
        dma((nt,)),
        dma((nt,)),
        dma((nt,)),
        dma((nt,)),
        dma((ns,)),
        dma((ns,)),
        dma((nz,)),
        dma((nz,)),
        dma((nz, nt)),
        dma((nz, nt)),
        dma((nz // 2, nt)),
        dma((nz // 2, nt)),
        dma((nz,)),
        dma((nz,)),
        dma((ns,)),
        dma((ns,)),
        dma((nt,)),
        dma((nt,)),
    ]
    in_vmem = pl.BlockSpec(memory_space=pltpu.VMEM)
    anywhere = pl.BlockSpec(memory_space=pl.ANY)
    out = pl.pallas_call(
        functools.partial(kernel, (nx, nz, nc, nt)),
        out_shape=jax.ShapeDtypeStruct((rows, width), BF16),
        in_specs=[pl.BlockSpec(memory_space=pltpu.SMEM)] + [in_vmem] * 5 + [anywhere] * 8,
        out_specs=in_vmem,
        scratch_shapes=scratch,
        compiler_params=pltpu.CompilerParams(
            collective_id=0, has_side_effects=True, vmem_limit_bytes=VMEM_LIMIT
        ),
        name="layer",
    )(
        lengths,
        new_keys[:, 0],
        new_values[:, 0],
        norm_gain[None],
        routes[0],
        route_weights[0],
        queries,
        cache_keys[:, 0],
        cache_values[:, 0],
        out_weight.T,
        residual[0],
        gate_weight[0],
        up_weight[0],
        down_weight[0],
    )
    return out[None]


def solution(mesh):
    placed = (
        P("ep", "tp", None),
        P("ep", "tp", None, None),
        P("ep", "tp", None, None),
        P("ep", "tp", None),
        P("ep", "tp", None),
        P("ep"),
        P("tp", "ep"),
        P("ep", "tp", None),
        P(),
        P("ep", "tp", None),
        P("ep", "tp", None),
        P("ep", None, "tp"),
        P("ep", None, "tp"),
        P("ep", "tp", None),
    )
    return jax.shard_map(
        functools.partial(on_device, mesh.shape["tp"]),
        mesh=mesh,
        in_specs=placed,
        out_specs=P("ep", "tp", None),
        check_vma=False,
    )
```

```python
import functools

import jax
import jax.numpy as jnp
from jax import lax
from jax.experimental import pallas as pl
from jax.experimental.pallas import tpu as pltpu
from jax.sharding import PartitionSpec as P

MESH = pl.DeviceIdType.MESH
BF16 = jnp.bfloat16
F32 = jnp.float32
EP_SHAPE = (4, 8, 2)
LANES = 128
CAP = 2
VMEM_LIMIT = 60 * 1024 * 1024


def dot(a, b):
    return jnp.dot(a, b, preferred_element_type=F32)


def dot_nt(a, b):
    return lax.dot_general(a, b, (((1,), (1,)), ((), ())), preferred_element_type=F32)


def offsets(nz):
    return {8: (0, -1, 2, -3, 4, 3, -2, 1), 4: (0, 2, 1, -1), 2: (0, 1)}[nz]


def offset_of(index, nz):
    value = jnp.zeros_like(index)
    for i, d in enumerate(offsets(nz)):
        value = jnp.where(index == i, d, value)
    return value


def kernel(
    dims,
    lengths_ref,
    nk_hbm,
    nv_hbm,
    gain_hbm,
    routes_hbm,
    shares_hbm,
    q_hbm,
    k_hbm,
    v_hbm,
    wt_hbm,
    res_hbm,
    gate_hbm,
    up_hbm,
    down_hbm,
    out_ref,
    nk_ref,
    nv_ref,
    gain_ref,
    routes_ref,
    shares_ref,
    q_buf,
    k_buf,
    v_buf,
    mixed_buf,
    wg,
    xg,
    rs_send,
    rs_recv,
    projg,
    resg,
    hid,
    info,
    comb,
    sel,
    xs,
    gu,
    dwg,
    actg,
    ret_send,
    ret_recv,
    early_sum,
    fin_send,
    fin_pair,
    fin_sum,
    fin_recv,
    fy_send,
    fy_recv,
    load_sem,
    ring_ss,
    ring_rs,
    x_ss,
    x_rs,
    res_ss,
    res_rs,
    info_ss,
    info_rs,
    infoy_ss,
    infoy_rs,
    dw_ss,
    dw_rs,
    rs_ss,
    rs_rs,
    proj_ss,
    proj_rs,
    sel_ss,
    sel_rs,
    xs_ss,
    xs_rs,
    far_ss,
    far_rs,
    act_ss,
    act_rs,
    ret_ss,
    ret_rs,
    fin_ss,
    fin_rs,
    fy_ss,
    fy_rs,
):
    nx, nz, nc, nt = dims
    ns = nx * nc
    rows = res_hbm.shape[0]
    width = res_hbm.shape[1]
    quarter = width // nt
    group_rows = nt * rows
    heads, head_size = q_buf.shape[1], q_buf.shape[2]
    context = k_hbm.shape[1]
    hidden_units = gate_hbm.shape[1]
    chunk = ns * CAP

    ep = lax.axis_index("ep")
    t = lax.axis_index("tp")
    x = ep // (nz * nc)
    z = (ep // nc) % nz
    c = ep % nc
    s = x * nc + c

    def z_peer(d):
        return {"ep": (x * nz + (z + d + nz) % nz) * nc + c, "tp": t}

    sibling = {"ep": (x * nz + z) * nc + 1 - c, "tp": t}

    def x_index(d):
        return (x + d) % nx

    def x_peer(d):
        return {"ep": (x_index(d) * nz + z) * nc + c, "tp": t}

    def t_index(d):
        return (t + d) % nt

    def t_peer(d):
        return {"ep": ep, "tp": t_index(d)}

    pending = []

    def describe(src, dst, sems, at, peer):
        return pltpu.make_async_remote_copy(
            src_ref=src,
            dst_ref=dst,
            send_sem=sems[0].at[at],
            recv_sem=sems[1].at[at],
            device_id=peer,
            device_id_type=MESH,
        )

    def send(src, dst, sems, at, peer):
        copy = describe(src, dst, sems, at, peer)
        copy.start()
        pending.append(copy)

    def arrive(dst, sems, at):
        describe(dst, dst, sems, at, t_peer(1)).wait_recv()

    def spread_start(view, sems, own=None, pre=()):
        own = view(s) if own is None else own
        for d in range(1, nx):
            send(own, view(s), sems, pre + (0, d), x_peer(d))
        send(own, view(s), sems, pre + (1, 0), sibling)

    def spread_relay(view, sems, pre=()):
        for d in range(1, nx):
            block = view(x_index(nx - d) * nc + c)
            arrive(block, sems, pre + (0, d))
            send(block, block, sems, pre + (1, d), sibling)

    def spread_end(view, sems, pre=()):
        for d in range(nx):
            arrive(view(x_index(nx - d) * nc + 1 - c), sems, pre + (1, d))

    barrier = pltpu.get_barrier_semaphore()
    partners = (
        [z_peer(d) for d in range(1, nz)]
        + [x_peer(d) for d in range(1, nx)]
        + [sibling]
        + [t_peer(d) for d in range(1, nt)]
    )
    for peer in partners:
        pl.semaphore_signal(barrier, inc=1, device_id=peer, device_id_type=MESH)

    def load(src, dst, n):
        copy = pltpu.make_async_copy(src, dst, load_sem.at[n])
        copy.start()
        return copy

    q_load = load(q_hbm, q_buf, 0)
    k_load = load(k_hbm, k_buf.at[:, pl.ds(0, context)], 1)
    v_load = load(v_hbm, v_buf.at[:, pl.ds(0, context)], 2)
    small_loads = [
        load(src, dst, 8 + n)
        for n, (src, dst) in enumerate(
            (
                (nk_hbm, nk_ref),
                (nv_hbm, nv_ref),
                (gain_hbm, gain_ref),
                (routes_hbm, routes_ref),
                (shares_hbm, shares_ref),
            )
        )
    ]
    w_load = load(wt_hbm, wg.at[nz - 2], 3)
    r_load = load(res_hbm, resg.at[s], 4)

    lane = lax.broadcasted_iota(jnp.int32, (rows, LANES), 1)
    row = lax.broadcasted_iota(jnp.int32, (rows, LANES), 0)
    member = jnp.zeros((rows, LANES), F32)
    share = jnp.zeros((rows, LANES), F32)
    for n in (3, 4):
        small_loads[n].wait()
    routes = routes_ref[...]
    shares = shares_ref[...]
    for k in range(routes.shape[1]):
        hit = routes[:, k : k + 1] == lane
        member = jnp.where(hit, 1.0, member)
        share = share + jnp.where(hit, shares[:, k : k + 1], 0.0)
    rank = jnp.zeros((rows, LANES), F32)
    for j in range(rows - 1):
        rank = rank + jnp.where(row > j, member[j : j + 1, :], 0.0)
    info[t, s, 0] = jnp.where(member > 0.0, rank, -1.0)
    info[t, s, 1] = share

    pl.semaphore_wait(barrier, len(partners))

    half = nz // 2
    wrows = wt_hbm.shape[0]
    top, low = pl.ds(0, wrows // 2), pl.ds(wrows // 2, wrows // 2)

    pieces = (top, low)

    def ring_slot(side, j):
        return nz - 1 if j == half else 2 * (j - 1) + side

    def ring_send(j, k):
        for side, d in enumerate((1, -1)):
            if j == half and k != side:
                continue
            src = wt_hbm if j == 1 else wg.at[ring_slot(side, j - 1)]
            dst = wg.at[ring_slot(side, j), pieces[k]]
            send(src.at[pieces[k]], dst, (ring_ss, ring_rs), (side, j - 1, k), z_peer(d))

    def ring_wait(j, k):
        for side in range(2):
            if j == half and k != side:
                continue
            dst = wg.at[ring_slot(side, j), pieces[k]]
            arrive(dst, (ring_ss, ring_rs), (side, j - 1, k))

    events = [(j, k) for j in range(1, half) for k in range(2)]

    def ring_event():
        if events:
            j, k = events.pop(0)
            ring_wait(j, k)
            ring_send(j + 1, k)

    for k in range(2):
        ring_send(1, k)

    def info_of(p):
        return info.at[t, p]

    def res_of(p):
        return resg.at[p]

    def x_of(p):
        return xg.at[p]

    spread_start(info_of, (info_ss, info_rs))
    spread_start(res_of, (res_ss, res_rs), res_hbm)
    unit_cut = hidden_units * 3 // 4

    unit_parts = (pl.ds(0, unit_cut), pl.ds(unit_cut, hidden_units - unit_cut))

    def send_down(k):
        for d in range(1, nt):
            part = pl.ds(pl.multiple_of(t_index(d) * quarter, LANES), quarter)
            units = unit_parts[k]
            send(down_hbm.at[units, part], dwg.at[t, units], (dw_ss, dw_rs), (k, d), t_peer(d))

    send_down(0)

    tail = k_buf.shape[1] - context
    at_slot = lax.broadcasted_iota(jnp.int32, (group_rows, tail, head_size), 1) == 0
    for n in (0, 1, 2):
        small_loads[n].wait()
    for buf, fresh in ((k_buf, nk_ref), (v_buf, nv_ref)):
        value = jnp.where(at_slot, fresh[...].astype(F32)[:, None, :], 0.0)
        buf[:, context:, :] = value.astype(BF16)
    q_load.wait()
    k_load.wait()
    v_load.wait()
    g_load = load(gate_hbm, gu.at[:, pl.ds(0, hidden_units)], 5)
    u_load = load(up_hbm, gu.at[:, pl.ds(hidden_units, hidden_units)], 6)
    my_quarter = pl.ds(pl.multiple_of(t * quarter, LANES), quarter)
    d_load = load(down_hbm.at[:, my_quarter], dwg.at[t], 7)
    scale = head_size ** (-0.5)
    step_rows = 8

    def attend(g):
        slot = lax.broadcasted_iota(jnp.int32, (heads, context + tail), 1)
        rows_here = [g * step_rows + j for j in range(step_rows)]
        scores = [dot_nt(q_buf[r], k_buf[r]) for r in rows_here]
        probs = []
        for r, score in zip(rows_here, scores):
            valid = (slot < lengths_ref[r]) | (slot == context)
            score = jnp.where(valid, score * scale, -1e30)
            weight = jnp.exp(score - jnp.max(score, axis=1, keepdims=True))
            total = jnp.sum(weight, axis=1, keepdims=True)
            probs.append((weight * (1.0 / total)).astype(BF16))
        for r, prob in zip(rows_here, probs):
            mixed_buf[r] = dot(prob, v_buf[r])

    for g in range(group_rows // step_rows):
        attend(g)
        ring_event()
    for h in range(heads):
        xg[s, :, h * head_size : (h + 1) * head_size] = mixed_buf[:, h, :].astype(BF16)
    spread_start(x_of, (x_ss, x_rs))
    spread_relay(info_of, (info_ss, info_rs))
    spread_relay(res_of, (res_ss, res_rs))
    spread_end(info_of, (info_ss, info_rs))
    for d in range(1, nt):
        send(info.at[t], info.at[t], (infoy_ss, infoy_rs), (d,), t_peer(d))

    picks = nz * chunk
    slot_no = lax.broadcasted_iota(jnp.int32, (picks, LANES), 0)
    at_z = (z + offset_of(slot_no // chunk, nz) + nz) % nz
    expert = (x * nz + at_z) * nc + c
    spread = (lax.broadcasted_iota(jnp.int32, (picks, LANES), 1) == expert).astype(BF16)
    code = info[t, :, 0].reshape(ns * rows, LANES).astype(BF16)
    seen = dot_nt(spread, code)
    slot_no = lax.broadcasted_iota(jnp.int32, (picks, ns * rows), 0)
    row_no = lax.broadcasted_iota(jnp.int32, (picks, ns * rows), 1)
    pick = (
        (seen == (slot_no % CAP).astype(F32)) & (row_no // rows == (slot_no % chunk) // CAP)
    ).astype(BF16)

    while events:
        ring_event()
    spread_relay(x_of, (x_ss, x_rs))
    spread_end(x_of, (x_ss, x_rs))

    nrow = ns * rows
    ncol = half * wrows
    all_rows = xg[...].reshape(ns * group_rows, xg.shape[2])

    def project(q):
        cols = wg[q * half : (q + 1) * half].reshape(ncol, wg.shape[2])
        part = dot_nt(all_rows, cols).reshape(ns, nt, rows, ncol)
        for tt in range(nt):
            rs_send[q, tt] = part[:, tt].reshape(nrow, ncol).astype(BF16)
        for d in range(1, nt):
            send(rs_send.at[q, t_index(d)], rs_recv.at[q, t], (rs_ss, rs_rs), (q, d), t_peer(d))

    def proj_of(q):
        return lambda p: projg.at[q, p]

    def gather(q):
        total = rs_send[q, t].astype(F32)
        for d in range(1, nt):
            p = t_index(nt - d)
            arrive(rs_recv.at[q, p], (rs_ss, rs_rs), (q, d))
            total = total + rs_recv[q, p].astype(F32)
        projg[q, s] = total.astype(BF16)
        spread_start(proj_of(q), (proj_ss, proj_rs), pre=(q,))

    w_load.wait()
    project(0)
    ring_wait(half, 0)
    ring_wait(half, 1)
    project(1)
    gather(0)
    gather(1)
    send_down(1)
    spread_end(res_of, (res_ss, res_rs))
    r_load.wait()

    left_half = lax.broadcasted_iota(jnp.int32, (nrow, LANES), 1) < wrows
    squares = jnp.zeros((nrow, LANES), F32)
    npair = ncol // LANES
    for q in range(2):
        spread_relay(proj_of(q), (proj_ss, proj_rs), pre=(q,))
        spread_end(proj_of(q), (proj_ss, proj_rs), pre=(q,))
        for m in range(npair):
            j = q * npair + m + 1
            blocks = ((z - j + nz) % nz, (z + j) % nz) if j < half else (z, (z + half) % nz)
            lanes = slice(m * LANES, (m + 1) * LANES)
            for xx in range(nx):
                a = projg[q, xx * nc, :, lanes].astype(F32)
                b = projg[q, xx * nc + 1, :, lanes].astype(F32)
                pair = (
                    jnp.where(left_half, a, pltpu.roll(b, wrows, 1)),
                    jnp.where(left_half, pltpu.roll(a, wrows, 1), b),
                )
                for side in range(2):
                    col = pl.ds(pl.multiple_of((xx * nz + blocks[side]) * LANES, LANES), LANES)
                    base = resg[:, :, col].astype(F32).reshape(nrow, LANES)
                    value = base + pair[side]
                    hid[:, col] = value
                    squares = squares + value * value
    inverse = lax.rsqrt(jnp.sum(squares, axis=1, keepdims=True) * (1.0 / width) + 1e-06)
    cstep = min(width, 512)
    gain = gain_ref[...].astype(F32)
    for b in range(width // cstep):
        cs = slice(b * cstep, (b + 1) * cstep)
        values = []
        for j in range(b * cstep // LANES, (b + 1) * cstep // LANES):
            value = hid[:, j * LANES : (j + 1) * LANES] * inverse * gain[j : j + 1, :]
            values.append(value.astype(BF16))
        picked = dot(pick, jnp.concatenate(values, axis=1)).astype(BF16)
        xs[t, 0, :, cs] = picked[:chunk]
        for i in range(1, nz):
            sel[i, :, cs] = picked[i * chunk : (i + 1) * chunk]

    def send_chunk(i):
        if i < nz:
            send(sel.at[i], xs.at[t, i], (sel_ss, sel_rs), (i,), z_peer(offsets(nz)[i]))

    for i in (1, 2):
        send_chunk(i)

    def forward(i):
        if i > 0:
            arrive(xs.at[t, i], (sel_ss, sel_rs), (i,))
            send_chunk(i + 2)
        for d in (1, nt - 1):
            send(xs.at[t, i], xs.at[t, i], (xs_ss, xs_rs), (i, d), t_peer(d))

    def relay(i):
        for k, d in enumerate((1, nt - 1)):
            arrive(xs.at[t_index(nt - d), i], (xs_ss, xs_rs), (i, d))
            part = xs.at[t_index(nt - d), i, :, pl.ds(k * (width // 2), width // 2)]
            send(part, part, (far_ss, far_rs), (i, k), t_peer(d))

    def complete(i):
        for k in range(2):
            part = xs.at[t_index(nt // 2), i, :, pl.ds(k * (width // 2), width // 2)]
            arrive(part, (far_ss, far_rs), (i, k))

    per = 2
    pairs = nz // per
    for i in range(min(2 * per, nz)):
        forward(i)
    for i in range(per):
        relay(i)

    for d in range(1, nt):
        arrive(info.at[t_index(-d + nt)], (infoy_ss, infoy_rs), (d,))
    places = nz * nt * chunk
    block = nt * chunk
    slot_no = lax.broadcasted_iota(jnp.int32, (LANES, places), 1)
    at_z = (z + offset_of(slot_no // block, nz) + nz) % nz
    expert = (x * nz + at_z) * nc + c
    spread = (lax.broadcasted_iota(jnp.int32, (LANES, places), 0) == expert).astype(BF16)
    for tt in range(nt):
        code = info[tt, :, 0].reshape(nrow, LANES).astype(BF16)
        weight = info[tt, :, 1].reshape(nrow, LANES).astype(BF16)
        seen = dot(code, spread)
        given = dot(weight, spread)
        slot_no = lax.broadcasted_iota(jnp.int32, (nrow, places), 1)
        row_no = lax.broadcasted_iota(jnp.int32, (nrow, places), 0) + tt * nrow
        fits = (seen == (slot_no % CAP).astype(F32)) & (row_no // rows == (slot_no % block) // CAP)
        comb[tt * nrow : (tt + 1) * nrow, :] = jnp.where(fits, given, 0.0).astype(BF16)

    g_load.wait()
    u_load.wait()

    prow = nt * per * chunk

    def first(p):
        for i in range(per * p, per * p + per):
            complete(i)
        slots = xs[:, per * p : per * p + per].reshape(prow, width)
        both = dot(slots, gu[...])
        gate, up = both[:, :hidden_units], both[:, hidden_units:]
        act = (gate / (1.0 + jnp.exp(-gate)) * up).astype(BF16)
        actg[t, p] = act
        for d in range(1, nt):
            send(actg.at[t, p], actg.at[t, p], (act_ss, act_rs), (p, d), t_peer(d))

    def second(p):
        if p == 0:
            d_load.wait()
            for d in range(1, nt):
                for k in range(2):
                    units = unit_parts[k]
                    arrive(dwg.at[t_index(-d + nt), units], (dw_ss, dw_rs), (k, d))
        for d in range(1, nt):
            arrive(actg.at[t_index(-d + nt), p], (act_ss, act_rs), (p, d))
        total = dot(actg[0, p], dwg[0])
        for tt in range(1, nt):
            total = total + dot(actg[tt, p], dwg[tt])
        total = total.astype(BF16).reshape(nt, per, chunk, quarter)
        for k in range(per):
            i = per * p + k
            value = total[:, k].reshape(nt * chunk, quarter)
            if i == 0:
                ret_recv[0] = value
            else:
                ret_send[i] = value
                send(ret_send.at[i], ret_recv.at[i], (ret_ss, ret_rs), (i), z_peer(-offsets(nz)[i]))

    for p in range(pairs):
        for k in range(per):
            if p < pairs - 2:
                forward(per * (p + 2) + k)
            if p < pairs - 1:
                relay(per * (p + 1) + k)
        first(p)
        if p > 0:
            second(p - 1)
    second(pairs - 1)

    early = nz - per
    for i in range(1, early):
        arrive(ret_recv.at[i], (ret_ss, ret_rs), (i,))
    back = ret_recv[:early].reshape(early * block, quarter)
    early_sum[...] = dot(comb[:, : early * block], back)
    for i in range(early, nz):
        arrive(ret_recv.at[i], (ret_ss, ret_rs), (i,))
    back = ret_recv[early:].reshape(per * block, quarter)
    for tt in range(nt):
        these = slice(tt * nrow, (tt + 1) * nrow)
        part = dot(comb[these, early * block :], back) + early_sum[these, :]
        part = part.reshape(nx, nc, rows, quarter).astype(BF16)
        for xx in range(nx):
            for cc in range(nc):
                fin_send[cc, xx, tt * rows : (tt + 1) * rows, :] = part[xx, cc]
    send(fin_send.at[1 - c], fin_pair, (fin_ss, fin_rs), (0,), sibling)
    arrive(fin_pair, (fin_ss, fin_rs), (0,))
    for d in range(1, nx):
        p = x_index(d)
        fin_sum[p] = (fin_send[c, p].astype(F32) + fin_pair[p].astype(F32)).astype(BF16)
        send(fin_sum.at[p], fin_recv.at[x], (fin_ss, fin_rs), (d,), x_peer(d))
    total = fin_send[c, x].astype(F32) + fin_pair[x].astype(F32)
    for d in range(1, nx):
        p = x_index(nx - d)
        arrive(fin_recv.at[p], (fin_ss, fin_rs), (d,))
        total = total + fin_recv[p].astype(F32)
    for tt in range(nt):
        fy_send[tt] = total[tt * rows : (tt + 1) * rows]
    for d in range(1, nt):
        send(fy_send.at[t_index(d)], fy_recv.at[t], (fy_ss, fy_rs), (d,), t_peer(d))
    fy_recv[t] = fy_send[t]
    for d in range(1, nt):
        arrive(fy_recv.at[t_index(-d + nt)], (fy_ss, fy_rs), (d,))
    own = pl.ds(pl.multiple_of(s * rows, rows), rows)
    for tt in range(nt):
        cs = slice(tt * quarter, (tt + 1) * quarter)
        out_ref[:, cs] = (hid[own, cs] + fy_recv[tt]).astype(BF16)
    for copy in pending:
        copy.wait_send()


def on_device(
    nt,
    queries,
    cache_keys,
    cache_values,
    new_keys,
    new_values,
    lengths,
    out_weight,
    residual,
    norm_gain,
    routes,
    route_weights,
    gate_weight,
    up_weight,
    down_weight,
):
    nx, nz, nc = EP_SHAPE
    ns = nx * nc
    group_rows, heads, head_size = queries.shape
    context = cache_keys.shape[2]
    flat = heads * head_size
    rows, width = residual.shape[1:]
    wcols = out_weight.shape[1]
    units = gate_weight.shape[2]
    quarter = width // nt
    chunk = ns * CAP
    nrow = ns * rows
    ncol = nz // 2 * wcols
    dma = pltpu.SemaphoreType.DMA
    vmem = pltpu.VMEM
    scratch = [
        vmem((group_rows, head_size), BF16),
        vmem((group_rows, head_size), BF16),
        vmem((width // LANES, LANES), BF16),
        vmem(routes.shape[1:], jnp.int32),
        vmem(routes.shape[1:], F32),
        vmem((group_rows, heads, head_size), BF16),
        vmem((group_rows, context + 16, head_size), BF16),
        vmem((group_rows, context + 16, head_size), BF16),
        vmem((group_rows, heads, head_size), F32),
        vmem((nz, wcols, flat), BF16),
        vmem((ns, group_rows, flat), BF16),
        vmem((2, nt, nrow, ncol), BF16),
        vmem((2, nt, nrow, ncol), BF16),
        vmem((2, ns, nrow, ncol), BF16),
        vmem((ns, rows, width), BF16),
        vmem((nrow, width), F32),
        vmem((nt, ns, 2, rows, LANES), F32),
        vmem((nt * nrow, nz * nt * chunk), BF16),
        vmem((nz, chunk, width), BF16),
        vmem((nt, nz, chunk, width), BF16),
        vmem((width, 2 * units), BF16),
        vmem((nt, units, quarter), BF16),
        vmem((nt, nz // 2, nt * 2 * chunk, units), BF16),
        vmem((nz, nt * chunk, quarter), BF16),
        vmem((nz, nt * chunk, quarter), BF16),
        vmem((nt * nrow, quarter), F32),
        vmem((nc, nx, group_rows, quarter), BF16),
        vmem((nx, group_rows, quarter), BF16),
        vmem((nx, group_rows, quarter), BF16),
        vmem((nx, group_rows, quarter), BF16),
        vmem((nt, rows, quarter), F32),
        vmem((nt, rows, quarter), F32),
        dma((13,)),
    ]
    for shape in (
        (2, nz // 2, 2),
        (2, nx),
        (2, nx),
        (2, nx),
        (nt,),
        (2, nt),
        (2, nt),
        (2, 2, nx),
        (nz,),
        (nz, nt),
        (nz, 2),
        (nz // 2, nt),
        (nz,),
        (nx,),
        (nt,),
    ):
        scratch += [dma(shape), dma(shape)]
    in_vmem = pl.BlockSpec(memory_space=pltpu.VMEM)
    anywhere = pl.BlockSpec(memory_space=pl.ANY)
    out = pl.pallas_call(
        functools.partial(kernel, (nx, nz, nc, nt)),
        out_shape=jax.ShapeDtypeStruct((rows, width), BF16),
        in_specs=[pl.BlockSpec(memory_space=pltpu.SMEM)] + [anywhere] * 13,
        out_specs=in_vmem,
        scratch_shapes=scratch,
        compiler_params=pltpu.CompilerParams(
            collective_id=0, has_side_effects=True, vmem_limit_bytes=VMEM_LIMIT
        ),
        name="layer",
    )(
        lengths,
        new_keys[:, 0],
        new_values[:, 0],
        norm_gain.reshape(width // LANES, LANES),
        routes[0],
        route_weights[0],
        queries,
        cache_keys[:, 0],
        cache_values[:, 0],
        out_weight.T,
        residual[0],
        gate_weight[0],
        up_weight[0],
        down_weight[0],
    )
    return out[None]


def solution(mesh):
    placed = (
        P("ep", "tp", None),
        P("ep", "tp", None, None),
        P("ep", "tp", None, None),
        P("ep", "tp", None),
        P("ep", "tp", None),
        P("ep"),
        P("tp", "ep"),
        P("ep", "tp", None),
        P(),
        P("ep", "tp", None),
        P("ep", "tp", None),
        P("ep", None, "tp"),
        P("ep", None, "tp"),
        P("ep", "tp", None),
    )
    return jax.shard_map(
        functools.partial(on_device, mesh.shape["tp"]),
        mesh=mesh,
        in_specs=placed,
        out_specs=P("ep", "tp", None),
        check_vma=False,
    )
```

```python
import functools

import jax
import jax.numpy as jnp
from jax import lax
from jax.experimental import pallas as pl
from jax.experimental.pallas import tpu as pltpu
from jax.sharding import PartitionSpec as P

MESH = pl.DeviceIdType.MESH
BF16 = jnp.bfloat16
F32 = jnp.float32
EP_SHAPE = (4, 8, 2)
LANES = 128
CAP = 2
VMEM_LIMIT = 60 * 1024 * 1024


def dot(a, b):
    return jnp.dot(a, b, preferred_element_type=F32)


def dot_nt(a, b):
    return lax.dot_general(a, b, (((1,), (1,)), ((), ())), preferred_element_type=F32)


def offsets(nz):
    return {8: (-1, 2, -3, 4, 3, -2, 1, 0), 4: (-1, 2, 1, 0)}[nz]


def offset_of(index, nz):
    value = jnp.zeros_like(index)
    for i, d in enumerate(offsets(nz)):
        value = jnp.where(index == i, d, value)
    return value


def kernel(
    dims,
    lengths_ref,
    nk_hbm,
    nv_hbm,
    gain_hbm,
    routes_hbm,
    shares_hbm,
    q_hbm,
    k_hbm,
    v_hbm,
    wt_hbm,
    res_hbm,
    gate_hbm,
    up_hbm,
    down_hbm,
    out_ref,
    nk_ref,
    nv_ref,
    gain_ref,
    routes_ref,
    shares_ref,
    q_buf,
    k_buf,
    v_buf,
    mixed_buf,
    wg,
    xg,
    rs_send,
    rs_recv,
    projg,
    resg,
    hid,
    info,
    comb,
    sel,
    xs,
    gu,
    dwg,
    actg,
    ret_send,
    ret_recv,
    early_sum,
    fin_send,
    fin_pair,
    fin_sum,
    fin_recv,
    fy_send,
    fy_recv,
    load_sem,
    ring_ss,
    ring_rs,
    x_ss,
    x_rs,
    res_ss,
    res_rs,
    info_ss,
    info_rs,
    infoy_ss,
    infoy_rs,
    dw_ss,
    dw_rs,
    rs_ss,
    rs_rs,
    proj_ss,
    proj_rs,
    sel_ss,
    sel_rs,
    xs_ss,
    xs_rs,
    far_ss,
    far_rs,
    act_ss,
    act_rs,
    afar_ss,
    afar_rs,
    ret_ss,
    ret_rs,
    fin_ss,
    fin_rs,
    fy_ss,
    fy_rs,
):
    nx, nz, nc, nt = dims
    ns = nx * nc
    rows = res_hbm.shape[0]
    width = res_hbm.shape[1]
    quarter = width // nt
    group_rows = nt * rows
    heads, head_size = q_buf.shape[1], q_buf.shape[2]
    context = k_hbm.shape[1]
    hidden_units = gate_hbm.shape[1]
    chunk = ns * CAP

    ep = lax.axis_index("ep")
    t = lax.axis_index("tp")
    x = ep // (nz * nc)
    z = (ep // nc) % nz
    c = ep % nc
    s = x * nc + c

    def z_peer(d):
        return {"ep": (x * nz + (z + d + nz) % nz) * nc + c, "tp": t}

    sibling = {"ep": (x * nz + z) * nc + 1 - c, "tp": t}

    def x_index(d):
        return (x + d) % nx

    def x_peer(d):
        return {"ep": (x_index(d) * nz + z) * nc + c, "tp": t}

    def t_index(d):
        return (t + d) % nt

    def t_peer(d):
        return {"ep": ep, "tp": t_index(d)}

    pending = []

    def describe(src, dst, sems, at, peer):
        return pltpu.make_async_remote_copy(
            src_ref=src,
            dst_ref=dst,
            send_sem=sems[0].at[at],
            recv_sem=sems[1].at[at],
            device_id=peer,
            device_id_type=MESH,
        )

    def send(src, dst, sems, at, peer):
        copy = describe(src, dst, sems, at, peer)
        copy.start()
        pending.append(copy)

    def arrive(dst, sems, at):
        describe(dst, dst, sems, at, t_peer(1)).wait_recv()

    def spread_start(view, sems, own=None, pre=()):
        own = view(s) if own is None else own
        for d in range(1, nx):
            send(own, view(s), sems, pre + (0, d), x_peer(d))
        send(own, view(s), sems, pre + (1, 0), sibling)

    def spread_relay(view, sems, pre=()):
        for d in range(1, nx):
            block = view(x_index(nx - d) * nc + c)
            arrive(block, sems, pre + (0, d))
            send(block, block, sems, pre + (1, d), sibling)

    def spread_end(view, sems, pre=()):
        for d in range(nx):
            arrive(view(x_index(nx - d) * nc + 1 - c), sems, pre + (1, d))

    barrier = pltpu.get_barrier_semaphore()
    partners = (
        [z_peer(d) for d in range(1, nz)]
        + [x_peer(d) for d in range(1, nx)]
        + [sibling]
        + [t_peer(d) for d in range(1, nt)]
    )
    for peer in partners:
        pl.semaphore_signal(barrier, inc=1, device_id=peer, device_id_type=MESH)

    def load(src, dst, n):
        copy = pltpu.make_async_copy(src, dst, load_sem.at[n])
        copy.start()
        return copy

    q_load = load(q_hbm, q_buf, 0)
    k_load = load(k_hbm, k_buf.at[:, pl.ds(0, context)], 1)
    v_load = load(v_hbm, v_buf.at[:, pl.ds(0, context)], 2)
    small_loads = [
        load(src, dst, 8 + n)
        for n, (src, dst) in enumerate(
            (
                (nk_hbm, nk_ref),
                (nv_hbm, nv_ref),
                (gain_hbm, gain_ref),
                (routes_hbm, routes_ref),
                (shares_hbm, shares_ref),
            )
        )
    ]
    w_load = load(wt_hbm, wg.at[nz - 2], 3)
    r_load = load(res_hbm, resg.at[s], 4)

    lane = lax.broadcasted_iota(jnp.int32, (rows, LANES), 1)
    row = lax.broadcasted_iota(jnp.int32, (rows, LANES), 0)
    member = jnp.zeros((rows, LANES), F32)
    share = jnp.zeros((rows, LANES), F32)
    for n in (3, 4):
        small_loads[n].wait()
    routes = routes_ref[...]
    shares = shares_ref[...]
    for k in range(routes.shape[1]):
        hit = routes[:, k : k + 1] == lane
        member = jnp.where(hit, 1.0, member)
        share = share + jnp.where(hit, shares[:, k : k + 1], 0.0)
    rank = jnp.zeros((rows, LANES), F32)
    for j in range(rows - 1):
        rank = rank + jnp.where(row > j, member[j : j + 1, :], 0.0)
    info[t, s, 0] = jnp.where(member > 0.0, rank, -1.0)
    info[t, s, 1] = share

    pl.semaphore_wait(barrier, len(partners))

    half = nz // 2
    wrows = wt_hbm.shape[0]
    top, low = pl.ds(0, wrows // 2), pl.ds(wrows // 2, wrows // 2)

    pieces = (top, low)

    def ring_slot(side, j):
        return nz - 1 if j == half else 2 * (j - 1) + side

    def ring_send(j, k):
        for side, d in enumerate((1, -1)):
            if j == half and k != side:
                continue
            src = wt_hbm if j == 1 else wg.at[ring_slot(side, j - 1)]
            dst = wg.at[ring_slot(side, j), pieces[k]]
            send(src.at[pieces[k]], dst, (ring_ss, ring_rs), (side, j - 1, k), z_peer(d))

    def ring_wait(j, k):
        for side in range(2):
            if j == half and k != side:
                continue
            dst = wg.at[ring_slot(side, j), pieces[k]]
            arrive(dst, (ring_ss, ring_rs), (side, j - 1, k))

    events = [(j, k) for j in range(1, half) for k in range(2)]

    def ring_event():
        if events:
            j, k = events.pop(0)
            ring_wait(j, k)
            ring_send(j + 1, k)

    for k in range(2):
        ring_send(1, k)

    def info_of(p):
        return info.at[t, p]

    def res_of(p):
        return resg.at[p]

    def x_of(p):
        return xg.at[p]

    spread_start(info_of, (info_ss, info_rs))
    spread_start(res_of, (res_ss, res_rs), res_hbm)
    unit_cut = hidden_units * 3 // 4

    unit_parts = (pl.ds(0, unit_cut), pl.ds(unit_cut, hidden_units - unit_cut))

    def send_down(k):
        for d in range(1, nt):
            part = pl.ds(pl.multiple_of(t_index(d) * quarter, LANES), quarter)
            units = unit_parts[k]
            send(down_hbm.at[units, part], dwg.at[t, units], (dw_ss, dw_rs), (k, d), t_peer(d))

    send_down(0)

    tail = k_buf.shape[1] - context
    at_slot = lax.broadcasted_iota(jnp.int32, (group_rows, tail, head_size), 1) == 0
    for n in (0, 1, 2):
        small_loads[n].wait()
    for buf, fresh in ((k_buf, nk_ref), (v_buf, nv_ref)):
        value = jnp.where(at_slot, fresh[...].astype(F32)[:, None, :], 0.0)
        buf[:, context:, :] = value.astype(BF16)
    q_load.wait()
    k_load.wait()
    v_load.wait()
    g_load = load(gate_hbm, gu.at[:, pl.ds(0, hidden_units)], 5)
    u_load = load(up_hbm, gu.at[:, pl.ds(hidden_units, hidden_units)], 6)
    my_quarter = pl.ds(pl.multiple_of(t * quarter, LANES), quarter)
    d_load = load(down_hbm.at[:, my_quarter], dwg.at[t], 7)
    scale = head_size ** (-0.5)
    step_rows = 8

    def attend(g):
        slot = lax.broadcasted_iota(jnp.int32, (heads, context + tail), 1)
        rows_here = [g * step_rows + j for j in range(step_rows)]
        scores = [dot_nt(q_buf[r], k_buf[r]) for r in rows_here]
        probs = []
        for r, score in zip(rows_here, scores):
            valid = (slot < lengths_ref[r]) | (slot == context)
            score = jnp.where(valid, score * scale, -1e30)
            weight = jnp.exp(score - jnp.max(score, axis=1, keepdims=True))
            total = jnp.sum(weight, axis=1, keepdims=True)
            probs.append((weight * (1.0 / total)).astype(BF16))
        for r, prob in zip(rows_here, probs):
            mixed_buf[r] = dot(prob, v_buf[r])

    for g in range(group_rows // step_rows):
        attend(g)
        ring_event()
    for h in range(heads):
        xg[s, :, h * head_size : (h + 1) * head_size] = mixed_buf[:, h, :].astype(BF16)
    spread_start(x_of, (x_ss, x_rs))
    spread_relay(info_of, (info_ss, info_rs))
    spread_relay(res_of, (res_ss, res_rs))
    spread_end(info_of, (info_ss, info_rs))
    for d in range(1, nt):
        send(info.at[t], info.at[t], (infoy_ss, infoy_rs), (d,), t_peer(d))

    picks = nz * chunk
    slot_no = lax.broadcasted_iota(jnp.int32, (picks, LANES), 0)
    at_z = (z + offset_of(slot_no // chunk, nz) + nz) % nz
    expert = (x * nz + at_z) * nc + c
    spread = (lax.broadcasted_iota(jnp.int32, (picks, LANES), 1) == expert).astype(BF16)
    code = info[t, :, 0].reshape(ns * rows, LANES).astype(BF16)
    seen = dot_nt(spread, code)
    slot_no = lax.broadcasted_iota(jnp.int32, (picks, ns * rows), 0)
    row_no = lax.broadcasted_iota(jnp.int32, (picks, ns * rows), 1)
    pick = (
        (seen == (slot_no % CAP).astype(F32)) & (row_no // rows == (slot_no % chunk) // CAP)
    ).astype(BF16)

    while events:
        ring_event()
    spread_relay(x_of, (x_ss, x_rs))
    spread_end(x_of, (x_ss, x_rs))

    nrow = ns * rows
    ncol = half * wrows
    all_rows = xg[...].reshape(ns * group_rows, xg.shape[2])

    def project(q):
        cols = wg[q * half : (q + 1) * half].reshape(ncol, wg.shape[2])
        part = dot_nt(all_rows, cols).reshape(ns, nt, rows, ncol)
        for tt in range(nt):
            rs_send[q, tt] = part[:, tt].reshape(nrow, ncol).astype(BF16)
        for d in range(1, nt):
            send(rs_send.at[q, t_index(d)], rs_recv.at[q, t], (rs_ss, rs_rs), (q, d), t_peer(d))

    def proj_of(q):
        return lambda p: projg.at[q, p]

    def gather(q):
        total = rs_send[q, t].astype(F32)
        for d in range(1, nt):
            p = t_index(nt - d)
            arrive(rs_recv.at[q, p], (rs_ss, rs_rs), (q, d))
            total = total + rs_recv[q, p].astype(F32)
        projg[q, s] = total.astype(BF16)
        spread_start(proj_of(q), (proj_ss, proj_rs), pre=(q,))

    w_load.wait()
    project(0)
    ring_wait(half, 0)
    ring_wait(half, 1)
    project(1)
    gather(0)
    gather(1)
    send_down(1)
    spread_end(res_of, (res_ss, res_rs))
    r_load.wait()

    left_half = lax.broadcasted_iota(jnp.int32, (nrow, LANES), 1) < wrows
    squares = jnp.zeros((nrow, LANES), F32)
    npair = ncol // LANES
    for q in range(2):
        spread_relay(proj_of(q), (proj_ss, proj_rs), pre=(q,))
        spread_end(proj_of(q), (proj_ss, proj_rs), pre=(q,))
        for m in range(npair):
            j = q * npair + m + 1
            blocks = ((z - j + nz) % nz, (z + j) % nz) if j < half else (z, (z + half) % nz)
            lanes = slice(m * LANES, (m + 1) * LANES)
            for xx in range(nx):
                a = projg[q, xx * nc, :, lanes].astype(F32)
                b = projg[q, xx * nc + 1, :, lanes].astype(F32)
                pair = (
                    jnp.where(left_half, a, pltpu.roll(b, wrows, 1)),
                    jnp.where(left_half, pltpu.roll(a, wrows, 1), b),
                )
                for side in range(2):
                    col = pl.ds(pl.multiple_of((xx * nz + blocks[side]) * LANES, LANES), LANES)
                    base = resg[:, :, col].astype(F32).reshape(nrow, LANES)
                    value = base + pair[side]
                    hid[:, col] = value
                    squares = squares + value * value
    inverse = lax.rsqrt(jnp.sum(squares, axis=1, keepdims=True) * (1.0 / width) + 1e-06)
    cstep = min(width, 512)
    gain = gain_ref[...].astype(F32)
    for b in range(width // cstep):
        cs = slice(b * cstep, (b + 1) * cstep)
        values = []
        for j in range(b * cstep // LANES, (b + 1) * cstep // LANES):
            value = hid[:, j * LANES : (j + 1) * LANES] * inverse * gain[j : j + 1, :]
            values.append(value.astype(BF16))
        picked = dot(pick, jnp.concatenate(values, axis=1)).astype(BF16)
        xs[t, nz - 1, :, cs] = picked[(nz - 1) * chunk :]
        for i in range(nz - 1):
            sel[i, :, cs] = picked[i * chunk : (i + 1) * chunk]

    def send_chunk(i):
        if i < nz - 1:
            send(sel.at[i], xs.at[t, i], (sel_ss, sel_rs), (i,), z_peer(offsets(nz)[i]))

    for i in (0, 1):
        send_chunk(i)

    def forward(i):
        if i < nz - 1:
            arrive(xs.at[t, i], (sel_ss, sel_rs), (i,))
            send_chunk(i + 2)
        for d in (1, nt - 1):
            send(xs.at[t, i], xs.at[t, i], (xs_ss, xs_rs), (i, d), t_peer(d))

    def relay(i):
        for k, d in enumerate((1, nt - 1)):
            arrive(xs.at[t_index(nt - d), i], (xs_ss, xs_rs), (i, d))
            part = xs.at[t_index(nt - d), i, :, pl.ds(k * (width // 2), width // 2)]
            send(part, part, (far_ss, far_rs), (i, k), t_peer(d))

    def complete(i):
        for k in range(2):
            part = xs.at[t_index(nt // 2), i, :, pl.ds(k * (width // 2), width // 2)]
            arrive(part, (far_ss, far_rs), (i, k))

    per = 2
    groups = [range(k, k + per) for k in range(0, nz - per, per)]
    groups += [range(k, k + 1) for k in range(nz - per, nz)]

    forward(nz - 1)
    forward(0)
    relay(nz - 1)
    forward(1)
    relay(0)

    for d in range(1, nt):
        arrive(info.at[t_index(-d + nt)], (infoy_ss, infoy_rs), (d,))
    places = nz * nt * chunk
    block = nt * chunk
    slot_no = lax.broadcasted_iota(jnp.int32, (LANES, places), 1)
    at_z = (z + offset_of(slot_no // block, nz) + nz) % nz
    expert = (x * nz + at_z) * nc + c
    spread = (lax.broadcasted_iota(jnp.int32, (LANES, places), 0) == expert).astype(BF16)
    for tt in range(nt):
        code = info[tt, :, 0].reshape(nrow, LANES).astype(BF16)
        weight = info[tt, :, 1].reshape(nrow, LANES).astype(BF16)
        seen = dot(code, spread)
        given = dot(weight, spread)
        slot_no = lax.broadcasted_iota(jnp.int32, (nrow, places), 1)
        row_no = lax.broadcasted_iota(jnp.int32, (nrow, places), 0) + tt * nrow
        fits = (seen == (slot_no % CAP).astype(F32)) & (row_no // rows == (slot_no % block) // CAP)
        comb[tt * nrow : (tt + 1) * nrow, :] = jnp.where(fits, given, 0.0).astype(BF16)

    g_load.wait()
    u_load.wait()

    def first(p):
        chunks = groups[p]
        count = len(chunks)
        these = pl.ds(chunks[0], count)
        for i in chunks:
            complete(i)
        slots = xs[:, chunks[0] : chunks[-1] + 1].reshape(nt * count * chunk, width)
        both = dot(slots, gu[...])
        gate, up = both[:, :hidden_units], both[:, hidden_units:]
        act = (gate / (1.0 + jnp.exp(-gate)) * up).reshape(nt, count, chunk, hidden_units)
        for k in range(count):
            actg[t, chunks[k]] = act[:, k].reshape(block, hidden_units).astype(BF16)
        part = actg.at[t, these]
        for d in (1, nt - 1) if count > 1 else range(1, nt):
            send(part, part, (act_ss, act_rs), (p, d), t_peer(d))

    def relay_act(p):
        for k, d in enumerate((1, nt - 1)):
            src = t_index(nt - d)
            arrive(actg.at[src, pl.ds(groups[p][0], per)], (act_ss, act_rs), (p, d))
            part = actg.at[src, groups[p][k]]
            send(part, part, (afar_ss, afar_rs), (p, k), t_peer(d))

    def second(p):
        chunks = groups[p]
        count = len(chunks)
        if p == 0:
            d_load.wait()
            for d in range(1, nt):
                for k in range(2):
                    units = unit_parts[k]
                    arrive(dwg.at[t_index(-d + nt), units], (dw_ss, dw_rs), (k, d))
        if count > 1:
            for k in range(per):
                arrive(actg.at[t_index(nt // 2), chunks[k]], (afar_ss, afar_rs), (p, k))
        else:
            for d in range(1, nt):
                arrive(actg.at[t_index(nt - d), pl.ds(chunks[0], 1)], (act_ss, act_rs), (p, d))
        total = jnp.zeros((count * block, quarter), F32)
        for tt in range(nt):
            part = actg[tt, chunks[0] : chunks[-1] + 1].reshape(count * block, hidden_units)
            total = total + dot(part, dwg[tt])
        for k, i in enumerate(chunks):
            value = total[k * block : (k + 1) * block].astype(BF16)
            if i == nz - 1:
                ret_recv[i] = value
            else:
                ret_send[i] = value
                send(
                    ret_send.at[i],
                    ret_recv.at[i],
                    (ret_ss, ret_rs),
                    (i,),
                    z_peer(-offsets(nz)[i]),
                )

    last = len(groups) - 1
    relay(1)
    forward(2)
    first(0)
    for p in range(1, last + 1):
        for i in range(per * p, min(per * p + per, nz - 1)):
            if i + 1 < nz - 1:
                forward(i + 1)
            relay(i)
        if len(groups[p - 1]) > 1:
            relay_act(p - 1)
        first(p)
        second(p - 1)

    early = nz - per
    for i in range(early):
        arrive(ret_recv.at[i], (ret_ss, ret_rs), (i,))
    back = ret_recv[:early].reshape(early * block, quarter)
    early_sum[...] = dot(comb[:, : early * block], back)
    second(last)
    for i in range(early, nz - 1):
        arrive(ret_recv.at[i], (ret_ss, ret_rs), (i,))
    back = ret_recv[early:].reshape(per * block, quarter)
    for tt in range(nt):
        these = slice(tt * nrow, (tt + 1) * nrow)
        part = dot(comb[these, early * block :], back) + early_sum[these, :]
        part = part.reshape(nx, nc, rows, quarter).astype(BF16)
        for xx in range(nx):
            for cc in range(nc):
                fin_send[cc, xx, tt * rows : (tt + 1) * rows, :] = part[xx, cc]
    send(fin_send.at[1 - c], fin_pair, (fin_ss, fin_rs), (0,), sibling)
    arrive(fin_pair, (fin_ss, fin_rs), (0,))
    for d in range(1, nx):
        p = x_index(d)
        fin_sum[p] = (fin_send[c, p].astype(F32) + fin_pair[p].astype(F32)).astype(BF16)
        send(fin_sum.at[p], fin_recv.at[x], (fin_ss, fin_rs), (d,), x_peer(d))
    total = fin_send[c, x].astype(F32) + fin_pair[x].astype(F32)
    for d in range(1, nx):
        p = x_index(nx - d)
        arrive(fin_recv.at[p], (fin_ss, fin_rs), (d,))
        total = total + fin_recv[p].astype(F32)
    for tt in range(nt):
        fy_send[tt] = total[tt * rows : (tt + 1) * rows]
    for d in range(1, nt):
        send(fy_send.at[t_index(d)], fy_recv.at[t], (fy_ss, fy_rs), (d,), t_peer(d))
    fy_recv[t] = fy_send[t]
    for d in range(1, nt):
        arrive(fy_recv.at[t_index(-d + nt)], (fy_ss, fy_rs), (d,))
    own = pl.ds(pl.multiple_of(s * rows, rows), rows)
    for tt in range(nt):
        cs = slice(tt * quarter, (tt + 1) * quarter)
        out_ref[:, cs] = (hid[own, cs] + fy_recv[tt]).astype(BF16)
    for copy in pending:
        copy.wait_send()


def on_device(
    nt,
    queries,
    cache_keys,
    cache_values,
    new_keys,
    new_values,
    lengths,
    out_weight,
    residual,
    norm_gain,
    routes,
    route_weights,
    gate_weight,
    up_weight,
    down_weight,
):
    nx, nz, nc = EP_SHAPE
    ns = nx * nc
    group_rows, heads, head_size = queries.shape
    context = cache_keys.shape[2]
    flat = heads * head_size
    rows, width = residual.shape[1:]
    wcols = out_weight.shape[1]
    units = gate_weight.shape[2]
    quarter = width // nt
    chunk = ns * CAP
    nrow = ns * rows
    ncol = nz // 2 * wcols
    dma = pltpu.SemaphoreType.DMA
    vmem = pltpu.VMEM
    scratch = [
        vmem((group_rows, head_size), BF16),
        vmem((group_rows, head_size), BF16),
        vmem((width // LANES, LANES), BF16),
        vmem(routes.shape[1:], jnp.int32),
        vmem(routes.shape[1:], F32),
        vmem((group_rows, heads, head_size), BF16),
        vmem((group_rows, context + 16, head_size), BF16),
        vmem((group_rows, context + 16, head_size), BF16),
        vmem((group_rows, heads, head_size), F32),
        vmem((nz, wcols, flat), BF16),
        vmem((ns, group_rows, flat), BF16),
        vmem((2, nt, nrow, ncol), BF16),
        vmem((2, nt, nrow, ncol), BF16),
        vmem((2, ns, nrow, ncol), BF16),
        vmem((ns, rows, width), BF16),
        vmem((nrow, width), F32),
        vmem((nt, ns, 2, rows, LANES), F32),
        vmem((nt * nrow, nz * nt * chunk), BF16),
        vmem((nz, chunk, width), BF16),
        vmem((nt, nz, chunk, width), BF16),
        vmem((width, 2 * units), BF16),
        vmem((nt, units, quarter), BF16),
        vmem((nt, nz, nt * chunk, units), BF16),
        vmem((nz, nt * chunk, quarter), BF16),
        vmem((nz, nt * chunk, quarter), BF16),
        vmem((nt * nrow, quarter), F32),
        vmem((nc, nx, group_rows, quarter), BF16),
        vmem((nx, group_rows, quarter), BF16),
        vmem((nx, group_rows, quarter), BF16),
        vmem((nx, group_rows, quarter), BF16),
        vmem((nt, rows, quarter), F32),
        vmem((nt, rows, quarter), F32),
        dma((13,)),
    ]
    for shape in (
        (2, nz // 2, 2),
        (2, nx),
        (2, nx),
        (2, nx),
        (nt,),
        (2, nt),
        (2, nt),
        (2, 2, nx),
        (nz,),
        (nz, nt),
        (nz, 2),
        (nz, nt),
        (nz // 2, 2),
        (nz,),
        (nx,),
        (nt,),
    ):
        scratch += [dma(shape), dma(shape)]
    in_vmem = pl.BlockSpec(memory_space=pltpu.VMEM)
    anywhere = pl.BlockSpec(memory_space=pl.ANY)
    out = pl.pallas_call(
        functools.partial(kernel, (nx, nz, nc, nt)),
        out_shape=jax.ShapeDtypeStruct((rows, width), BF16),
        in_specs=[pl.BlockSpec(memory_space=pltpu.SMEM)] + [anywhere] * 13,
        out_specs=in_vmem,
        scratch_shapes=scratch,
        compiler_params=pltpu.CompilerParams(
            collective_id=0, has_side_effects=True, vmem_limit_bytes=VMEM_LIMIT
        ),
        name="layer",
    )(
        lengths,
        new_keys[:, 0],
        new_values[:, 0],
        norm_gain.reshape(width // LANES, LANES),
        routes[0],
        route_weights[0],
        queries,
        cache_keys[:, 0],
        cache_values[:, 0],
        out_weight.T,
        residual[0],
        gate_weight[0],
        up_weight[0],
        down_weight[0],
    )
    return out[None]


def solution(mesh):
    placed = (
        P("ep", "tp", None),
        P("ep", "tp", None, None),
        P("ep", "tp", None, None),
        P("ep", "tp", None),
        P("ep", "tp", None),
        P("ep"),
        P("tp", "ep"),
        P("ep", "tp", None),
        P(),
        P("ep", "tp", None),
        P("ep", "tp", None),
        P("ep", None, "tp"),
        P("ep", None, "tp"),
        P("ep", "tp", None),
    )
    return jax.shard_map(
        functools.partial(on_device, mesh.shape["tp"]),
        mesh=mesh,
        in_specs=placed,
        out_specs=P("ep", "tp", None),
        check_vma=False,
    )
```

```python
import functools

import jax
import jax.numpy as jnp
from jax import lax
from jax.experimental import pallas as pl
from jax.experimental.pallas import tpu as pltpu
from jax.sharding import PartitionSpec as P

MESH = pl.DeviceIdType.MESH
BF16 = jnp.bfloat16
F32 = jnp.float32
EP_SHAPE = (4, 8, 2)
LANES = 128
CAP = 2
VMEM_LIMIT = 60 * 1024 * 1024


def dot(a, b):
    return jnp.dot(a, b, preferred_element_type=F32)


def dot_nt(a, b):
    return lax.dot_general(a, b, (((1,), (1,)), ((), ())), preferred_element_type=F32)


def offsets(nz):
    return {8: (-1, 2, -3, 4, 3, -2, 1, 0), 4: (-1, 2, 1, 0)}[nz]


def offset_of(index, nz):
    value = jnp.zeros_like(index)
    for i, d in enumerate(offsets(nz)):
        value = jnp.where(index == i, d, value)
    return value


def kernel(
    dims,
    lengths_ref,
    nk_hbm,
    nv_hbm,
    gain_hbm,
    routes_hbm,
    shares_hbm,
    q_hbm,
    k_hbm,
    v_hbm,
    wt_hbm,
    res_hbm,
    gate_hbm,
    up_hbm,
    down_hbm,
    out_ref,
    nk_ref,
    nv_ref,
    gain_ref,
    routes_ref,
    shares_ref,
    q_buf,
    k_buf,
    v_buf,
    mixed_buf,
    wg,
    xg,
    rs_send,
    rs_recv,
    projg,
    resg,
    hid,
    info,
    comb,
    sel,
    xs,
    gu,
    dwg,
    actg,
    ret_send,
    ret_recv,
    early_sum,
    fin_send,
    fin_pair,
    fin_sum,
    fin_recv,
    fy_send,
    fy_recv,
    load_sem,
    ring_ss,
    ring_rs,
    x_ss,
    x_rs,
    res_ss,
    res_rs,
    info_ss,
    info_rs,
    infoy_ss,
    infoy_rs,
    dw_ss,
    dw_rs,
    rs_ss,
    rs_rs,
    proj_ss,
    proj_rs,
    sel_ss,
    sel_rs,
    xs_ss,
    xs_rs,
    far_ss,
    far_rs,
    act_ss,
    act_rs,
    afar_ss,
    afar_rs,
    ret_ss,
    ret_rs,
    fin_ss,
    fin_rs,
    fy_ss,
    fy_rs,
):
    nx, nz, nc, nt = dims
    ns = nx * nc
    rows = res_hbm.shape[0]
    width = res_hbm.shape[1]
    quarter = width // nt
    group_rows = nt * rows
    heads, head_size = q_buf.shape[1], q_buf.shape[2]
    context = k_hbm.shape[1]
    hidden_units = gate_hbm.shape[1]
    chunk = ns * CAP

    ep = lax.axis_index("ep")
    t = lax.axis_index("tp")
    x = ep // (nz * nc)
    z = (ep // nc) % nz
    c = ep % nc
    s = x * nc + c

    def z_peer(d):
        return {"ep": (x * nz + (z + d + nz) % nz) * nc + c, "tp": t}

    sibling = {"ep": (x * nz + z) * nc + 1 - c, "tp": t}

    def x_index(d):
        return (x + d) % nx

    def x_peer(d):
        return {"ep": (x_index(d) * nz + z) * nc + c, "tp": t}

    def t_index(d):
        return (t + d) % nt

    def t_peer(d):
        return {"ep": ep, "tp": t_index(d)}

    pending = []

    def describe(src, dst, sems, at, peer):
        return pltpu.make_async_remote_copy(
            src_ref=src,
            dst_ref=dst,
            send_sem=sems[0].at[at],
            recv_sem=sems[1].at[at],
            device_id=peer,
            device_id_type=MESH,
        )

    def send(src, dst, sems, at, peer):
        copy = describe(src, dst, sems, at, peer)
        copy.start()
        pending.append(copy)

    def arrive(dst, sems, at):
        describe(dst, dst, sems, at, t_peer(1)).wait_recv()

    def spread_start(view, sems, own=None, pre=()):
        own = view(s) if own is None else own
        for d in range(1, nx):
            send(own, view(s), sems, pre + (0, d), x_peer(d))
        send(own, view(s), sems, pre + (1, 0), sibling)

    def spread_relay(view, sems, pre=()):
        for d in range(1, nx):
            block = view(x_index(nx - d) * nc + c)
            arrive(block, sems, pre + (0, d))
            send(block, block, sems, pre + (1, d), sibling)

    def spread_end(view, sems, pre=()):
        for d in range(nx):
            arrive(view(x_index(nx - d) * nc + 1 - c), sems, pre + (1, d))

    barrier = pltpu.get_barrier_semaphore()
    partners = (
        [z_peer(d) for d in (1, -1)]
        + [x_peer(d) for d in range(1, nx)]
        + [sibling]
        + [t_peer(d) for d in range(1, nt)]
    )
    for peer in partners:
        pl.semaphore_signal(barrier, inc=1, device_id=peer, device_id_type=MESH)

    def load(src, dst, n):
        copy = pltpu.make_async_copy(src, dst, load_sem.at[n])
        copy.start()
        return copy

    q_load = load(q_hbm, q_buf, 0)
    k_load = load(k_hbm, k_buf.at[:, pl.ds(0, context)], 1)
    v_load = load(v_hbm, v_buf.at[:, pl.ds(0, context)], 2)
    small_loads = [
        load(src, dst, 8 + n)
        for n, (src, dst) in enumerate(
            (
                (nk_hbm, nk_ref),
                (nv_hbm, nv_ref),
                (gain_hbm, gain_ref),
                (routes_hbm, routes_ref),
                (shares_hbm, shares_ref),
            )
        )
    ]
    w_load = load(wt_hbm, wg.at[nz - 2], 3)
    r_load = load(res_hbm, resg.at[s], 4)

    lane = lax.broadcasted_iota(jnp.int32, (rows, LANES), 1)
    row = lax.broadcasted_iota(jnp.int32, (rows, LANES), 0)
    member = jnp.zeros((rows, LANES), F32)
    share = jnp.zeros((rows, LANES), F32)
    for n in (3, 4):
        small_loads[n].wait()
    routes = routes_ref[...]
    shares = shares_ref[...]
    for k in range(routes.shape[1]):
        hit = routes[:, k : k + 1] == lane
        member = jnp.where(hit, 1.0, member)
        share = share + jnp.where(hit, shares[:, k : k + 1], 0.0)
    rank = jnp.zeros((rows, LANES), F32)
    for j in range(rows - 1):
        rank = rank + jnp.where(row > j, member[j : j + 1, :], 0.0)
    info[t, s, 0] = jnp.where(member > 0.0, rank, -1.0)
    info[t, s, 1] = share

    pl.semaphore_wait(barrier, len(partners))

    half = nz // 2
    wrows = wt_hbm.shape[0]
    top, low = pl.ds(0, wrows // 2), pl.ds(wrows // 2, wrows // 2)

    pieces = (top, low)

    def ring_slot(side, j):
        return nz - 1 if j == half else 2 * (j - 1) + side

    def ring_send(j, k):
        for side, d in enumerate((1, -1)):
            if j == half and k != side:
                continue
            src = wt_hbm if j == 1 else wg.at[ring_slot(side, j - 1)]
            dst = wg.at[ring_slot(side, j), pieces[k]]
            send(src.at[pieces[k]], dst, (ring_ss, ring_rs), (side, j - 1, k), z_peer(d))

    def ring_wait(j, k):
        for side in range(2):
            if j == half and k != side:
                continue
            dst = wg.at[ring_slot(side, j), pieces[k]]
            arrive(dst, (ring_ss, ring_rs), (side, j - 1, k))

    events = [(j, k) for j in range(1, half) for k in range(2)]

    def ring_event():
        if events:
            j, k = events.pop(0)
            ring_wait(j, k)
            ring_send(j + 1, k)

    for k in range(2):
        ring_send(1, k)

    def info_of(p):
        return info.at[t, p]

    def res_of(p):
        return resg.at[p]

    def x_of(p):
        return xg.at[p]

    spread_start(info_of, (info_ss, info_rs))
    spread_start(res_of, (res_ss, res_rs), res_hbm)
    unit_cut = hidden_units * 3 // 4

    unit_parts = (pl.ds(0, unit_cut), pl.ds(unit_cut, hidden_units - unit_cut))

    def send_down(k):
        for d in range(1, nt):
            part = pl.ds(pl.multiple_of(t_index(d) * quarter, LANES), quarter)
            units = unit_parts[k]
            send(down_hbm.at[units, part], dwg.at[t, units], (dw_ss, dw_rs), (k, d), t_peer(d))

    send_down(0)

    tail = k_buf.shape[1] - context
    at_slot = lax.broadcasted_iota(jnp.int32, (group_rows, tail, head_size), 1) == 0
    for n in (0, 1, 2):
        small_loads[n].wait()
    for buf, fresh in ((k_buf, nk_ref), (v_buf, nv_ref)):
        value = jnp.where(at_slot, fresh[...].astype(F32)[:, None, :], 0.0)
        buf[:, context:, :] = value.astype(BF16)
    q_load.wait()
    k_load.wait()
    v_load.wait()
    g_load = load(gate_hbm, gu.at[:, pl.ds(0, hidden_units)], 5)
    u_load = load(up_hbm, gu.at[:, pl.ds(hidden_units, hidden_units)], 6)
    my_quarter = pl.ds(pl.multiple_of(t * quarter, LANES), quarter)
    d_load = load(down_hbm.at[:, my_quarter], dwg.at[t], 7)
    scale = head_size ** (-0.5)
    step_rows = 8

    def attend(g):
        slot = lax.broadcasted_iota(jnp.int32, (heads, context + tail), 1)
        rows_here = [g * step_rows + j for j in range(step_rows)]
        scores = [dot_nt(q_buf[r], k_buf[r]) for r in rows_here]
        probs = []
        for r, score in zip(rows_here, scores):
            valid = (slot < lengths_ref[r]) | (slot == context)
            score = jnp.where(valid, score * scale, -1e30)
            weight = jnp.exp(score - jnp.max(score, axis=1, keepdims=True))
            total = jnp.sum(weight, axis=1, keepdims=True)
            probs.append((weight * (1.0 / total)).astype(BF16))
        for r, prob in zip(rows_here, probs):
            mixed_buf[r] = dot(prob, v_buf[r])

    for g in range(group_rows // step_rows):
        attend(g)
        ring_event()
    for h in range(heads):
        xg[s, :, h * head_size : (h + 1) * head_size] = mixed_buf[:, h, :].astype(BF16)
    spread_start(x_of, (x_ss, x_rs))
    spread_relay(info_of, (info_ss, info_rs))
    spread_relay(res_of, (res_ss, res_rs))
    spread_end(info_of, (info_ss, info_rs))
    for d in range(1, nt):
        send(info.at[t], info.at[t], (infoy_ss, infoy_rs), (d,), t_peer(d))

    picks = nz * chunk
    slot_no = lax.broadcasted_iota(jnp.int32, (picks, LANES), 0)
    at_z = (z + offset_of(slot_no // chunk, nz) + nz) % nz
    expert = (x * nz + at_z) * nc + c
    spread = (lax.broadcasted_iota(jnp.int32, (picks, LANES), 1) == expert).astype(BF16)
    code = info[t, :, 0].reshape(ns * rows, LANES).astype(BF16)
    seen = dot_nt(spread, code)
    slot_no = lax.broadcasted_iota(jnp.int32, (picks, ns * rows), 0)
    row_no = lax.broadcasted_iota(jnp.int32, (picks, ns * rows), 1)
    pick = (
        (seen == (slot_no % CAP).astype(F32)) & (row_no // rows == (slot_no % chunk) // CAP)
    ).astype(BF16)

    while events:
        ring_event()
    spread_relay(x_of, (x_ss, x_rs))
    spread_end(x_of, (x_ss, x_rs))

    nrow = ns * rows
    ncol = half * wrows
    all_rows = xg[...].reshape(ns * group_rows, xg.shape[2])

    def project(q):
        cols = wg[q * half : (q + 1) * half].reshape(ncol, wg.shape[2])
        part = dot_nt(all_rows, cols).reshape(ns, nt, rows, ncol)
        for tt in range(nt):
            rs_send[q, tt] = part[:, tt].reshape(nrow, ncol).astype(BF16)
        for d in range(1, nt):
            send(rs_send.at[q, t_index(d)], rs_recv.at[q, t], (rs_ss, rs_rs), (q, d), t_peer(d))

    def proj_of(q):
        return lambda p: projg.at[q, p]

    def gather(q):
        total = rs_send[q, t].astype(F32)
        for d in range(1, nt):
            p = t_index(nt - d)
            arrive(rs_recv.at[q, p], (rs_ss, rs_rs), (q, d))
            total = total + rs_recv[q, p].astype(F32)
        projg[q, s] = total.astype(BF16)
        spread_start(proj_of(q), (proj_ss, proj_rs), pre=(q,))

    w_load.wait()
    project(0)
    ring_wait(half, 0)
    ring_wait(half, 1)
    project(1)
    gather(0)
    gather(1)
    send_down(1)
    spread_end(res_of, (res_ss, res_rs))
    r_load.wait()

    left_half = lax.broadcasted_iota(jnp.int32, (nrow, LANES), 1) < wrows
    squares = jnp.zeros((nrow, LANES), F32)
    npair = ncol // LANES
    for q in range(2):
        spread_relay(proj_of(q), (proj_ss, proj_rs), pre=(q,))
        spread_end(proj_of(q), (proj_ss, proj_rs), pre=(q,))
        for m in range(npair):
            j = q * npair + m + 1
            blocks = ((z - j + nz) % nz, (z + j) % nz) if j < half else (z, (z + half) % nz)
            lanes = slice(m * LANES, (m + 1) * LANES)
            for xx in range(nx):
                a = projg[q, xx * nc, :, lanes].astype(F32)
                b = projg[q, xx * nc + 1, :, lanes].astype(F32)
                pair = (
                    jnp.where(left_half, a, pltpu.roll(b, wrows, 1)),
                    jnp.where(left_half, pltpu.roll(a, wrows, 1), b),
                )
                for side in range(2):
                    col = pl.ds(pl.multiple_of((xx * nz + blocks[side]) * LANES, LANES), LANES)
                    base = resg[:, :, col].astype(F32).reshape(nrow, LANES)
                    value = base + pair[side]
                    hid[:, col] = value
                    squares = squares + value * value
    inverse = lax.rsqrt(jnp.sum(squares, axis=1, keepdims=True) * (1.0 / width) + 1e-06)
    cstep = min(width, 512)
    gain = gain_ref[...].astype(F32)
    for b in range(width // cstep):
        cs = slice(b * cstep, (b + 1) * cstep)
        values = []
        for j in range(b * cstep // LANES, (b + 1) * cstep // LANES):
            value = hid[:, j * LANES : (j + 1) * LANES] * inverse * gain[j : j + 1, :]
            values.append(value.astype(BF16))
        picked = dot(pick, jnp.concatenate(values, axis=1)).astype(BF16)
        xs[t, nz - 1, :, cs] = picked[(nz - 1) * chunk :]
        for i in range(nz - 1):
            sel[i, :, cs] = picked[i * chunk : (i + 1) * chunk]

    def send_chunk(i):
        if i < nz - 1:
            send(sel.at[i], xs.at[t, i], (sel_ss, sel_rs), (i,), z_peer(offsets(nz)[i]))

    for i in (0, 1):
        send_chunk(i)

    def forward(i):
        if i < nz - 1:
            arrive(xs.at[t, i], (sel_ss, sel_rs), (i,))
            send_chunk(i + 2)
        for d in (1, nt - 1):
            send(xs.at[t, i], xs.at[t, i], (xs_ss, xs_rs), (i, d), t_peer(d))

    def relay(i):
        for k, d in enumerate((1, nt - 1)):
            arrive(xs.at[t_index(nt - d), i], (xs_ss, xs_rs), (i, d))
            part = xs.at[t_index(nt - d), i, :, pl.ds(k * (width // 2), width // 2)]
            send(part, part, (far_ss, far_rs), (i, k), t_peer(d))

    def complete(i):
        for k in range(2):
            part = xs.at[t_index(nt // 2), i, :, pl.ds(k * (width // 2), width // 2)]
            arrive(part, (far_ss, far_rs), (i, k))

    per = 2
    groups = [range(k, k + per) for k in range(0, nz - per, per)]
    groups += [range(k, k + 1) for k in range(nz - per, nz)]

    forward(nz - 1)
    forward(0)
    relay(nz - 1)
    forward(1)
    relay(0)

    for d in range(1, nt):
        arrive(info.at[t_index(-d + nt)], (infoy_ss, infoy_rs), (d,))
    places = nz * nt * chunk
    block = nt * chunk
    slot_no = lax.broadcasted_iota(jnp.int32, (LANES, places), 1)
    at_z = (z + offset_of(slot_no // block, nz) + nz) % nz
    expert = (x * nz + at_z) * nc + c
    spread = (lax.broadcasted_iota(jnp.int32, (LANES, places), 0) == expert).astype(BF16)
    for tt in range(nt):
        code = info[tt, :, 0].reshape(nrow, LANES).astype(BF16)
        weight = info[tt, :, 1].reshape(nrow, LANES).astype(BF16)
        seen = dot(code, spread)
        given = dot(weight, spread)
        slot_no = lax.broadcasted_iota(jnp.int32, (nrow, places), 1)
        row_no = lax.broadcasted_iota(jnp.int32, (nrow, places), 0) + tt * nrow
        fits = (seen == (slot_no % CAP).astype(F32)) & (row_no // rows == (slot_no % block) // CAP)
        comb[tt * nrow : (tt + 1) * nrow, :] = jnp.where(fits, given, 0.0).astype(BF16)

    g_load.wait()
    u_load.wait()

    def first(p):
        chunks = groups[p]
        count = len(chunks)
        these = pl.ds(chunks[0], count)
        for i in chunks:
            complete(i)
        slots = xs[:, chunks[0] : chunks[-1] + 1].reshape(nt * count * chunk, width)
        both = dot(slots, gu[...])
        gate, up = both[:, :hidden_units], both[:, hidden_units:]
        act = (gate / (1.0 + jnp.exp(-gate)) * up).reshape(nt, count, chunk, hidden_units)
        for k in range(count):
            actg[t, chunks[k]] = act[:, k].reshape(block, hidden_units).astype(BF16)
        part = actg.at[t, these]
        for d in (1, nt - 1) if count > 1 else range(1, nt):
            send(part, part, (act_ss, act_rs), (p, d), t_peer(d))

    def relay_act(p):
        for k, d in enumerate((1, nt - 1)):
            src = t_index(nt - d)
            arrive(actg.at[src, pl.ds(groups[p][0], per)], (act_ss, act_rs), (p, d))
            part = actg.at[src, groups[p][k]]
            send(part, part, (afar_ss, afar_rs), (p, k), t_peer(d))

    def second(p):
        chunks = groups[p]
        count = len(chunks)
        if p == 0:
            d_load.wait()
            for d in range(1, nt):
                for k in range(2):
                    units = unit_parts[k]
                    arrive(dwg.at[t_index(-d + nt), units], (dw_ss, dw_rs), (k, d))
        if count > 1:
            for k in range(per):
                arrive(actg.at[t_index(nt // 2), chunks[k]], (afar_ss, afar_rs), (p, k))
        else:
            for d in range(1, nt):
                arrive(actg.at[t_index(nt - d), pl.ds(chunks[0], 1)], (act_ss, act_rs), (p, d))
        total = jnp.zeros((count * block, quarter), F32)
        for tt in range(nt):
            part = actg[tt, chunks[0] : chunks[-1] + 1].reshape(count * block, hidden_units)
            total = total + dot(part, dwg[tt])
        for k, i in enumerate(chunks):
            value = total[k * block : (k + 1) * block].astype(BF16)
            if i == nz - 1:
                ret_recv[i] = value
            else:
                ret_send[i] = value
                send(
                    ret_send.at[i],
                    ret_recv.at[i],
                    (ret_ss, ret_rs),
                    (i,),
                    z_peer(-offsets(nz)[i]),
                )

    last = len(groups) - 1
    relay(1)
    forward(2)
    first(0)
    for p in range(1, last + 1):
        for i in range(per * p, min(per * p + per, nz - 1)):
            if i + 1 < nz - 1:
                forward(i + 1)
            relay(i)
        if len(groups[p - 1]) > 1:
            relay_act(p - 1)
        first(p)
        second(p - 1)

    early = nz - per
    for i in range(early):
        arrive(ret_recv.at[i], (ret_ss, ret_rs), (i,))
    back = ret_recv[:early].reshape(early * block, quarter)
    early_sum[...] = dot(comb[:, : early * block], back)
    second(last)
    for i in range(early, nz - 1):
        arrive(ret_recv.at[i], (ret_ss, ret_rs), (i,))
    back = ret_recv[early:].reshape(per * block, quarter)
    for tt in range(nt):
        these = slice(tt * nrow, (tt + 1) * nrow)
        part = dot(comb[these, early * block :], back) + early_sum[these, :]
        part = part.reshape(nx, nc, rows, quarter).astype(BF16)
        for xx in range(nx):
            for cc in range(nc):
                fin_send[cc, xx, tt * rows : (tt + 1) * rows, :] = part[xx, cc]
    send(fin_send.at[1 - c], fin_pair, (fin_ss, fin_rs), (0,), sibling)
    arrive(fin_pair, (fin_ss, fin_rs), (0,))
    for d in range(1, nx):
        p = x_index(d)
        fin_sum[p] = (fin_send[c, p].astype(F32) + fin_pair[p].astype(F32)).astype(BF16)
        send(fin_sum.at[p], fin_recv.at[x], (fin_ss, fin_rs), (d,), x_peer(d))
    total = fin_send[c, x].astype(F32) + fin_pair[x].astype(F32)
    for d in range(1, nx):
        p = x_index(nx - d)
        arrive(fin_recv.at[p], (fin_ss, fin_rs), (d,))
        total = total + fin_recv[p].astype(F32)
    for tt in range(nt):
        fy_send[tt] = total[tt * rows : (tt + 1) * rows]
    for d in range(1, nt):
        send(fy_send.at[t_index(d)], fy_recv.at[t], (fy_ss, fy_rs), (d,), t_peer(d))
    fy_recv[t] = fy_send[t]
    for d in range(1, nt):
        arrive(fy_recv.at[t_index(-d + nt)], (fy_ss, fy_rs), (d,))
    own = pl.ds(pl.multiple_of(s * rows, rows), rows)
    for tt in range(nt):
        cs = slice(tt * quarter, (tt + 1) * quarter)
        out_ref[:, cs] = (hid[own, cs] + fy_recv[tt]).astype(BF16)
    for copy in pending:
        copy.wait_send()


def on_device(
    nt,
    queries,
    cache_keys,
    cache_values,
    new_keys,
    new_values,
    lengths,
    out_weight,
    residual,
    norm_gain,
    routes,
    route_weights,
    gate_weight,
    up_weight,
    down_weight,
):
    nx, nz, nc = EP_SHAPE
    ns = nx * nc
    group_rows, heads, head_size = queries.shape
    context = cache_keys.shape[2]
    flat = heads * head_size
    rows, width = residual.shape[1:]
    wcols = out_weight.shape[1]
    units = gate_weight.shape[2]
    quarter = width // nt
    chunk = ns * CAP
    nrow = ns * rows
    ncol = nz // 2 * wcols
    dma = pltpu.SemaphoreType.DMA
    vmem = pltpu.VMEM
    scratch = [
        vmem((group_rows, head_size), BF16),
        vmem((group_rows, head_size), BF16),
        vmem((width // LANES, LANES), BF16),
        vmem(routes.shape[1:], jnp.int32),
        vmem(routes.shape[1:], F32),
        vmem((group_rows, heads, head_size), BF16),
        vmem((group_rows, context + 16, head_size), BF16),
        vmem((group_rows, context + 16, head_size), BF16),
        vmem((group_rows, heads, head_size), F32),
        vmem((nz, wcols, flat), BF16),
        vmem((ns, group_rows, flat), BF16),
        vmem((2, nt, nrow, ncol), BF16),
        vmem((2, nt, nrow, ncol), BF16),
        vmem((2, ns, nrow, ncol), BF16),
        vmem((ns, rows, width), BF16),
        vmem((nrow, width), F32),
        vmem((nt, ns, 2, rows, LANES), F32),
        vmem((nt * nrow, nz * nt * chunk), BF16),
        vmem((nz, chunk, width), BF16),
        vmem((nt, nz, chunk, width), BF16),
        vmem((width, 2 * units), BF16),
        vmem((nt, units, quarter), BF16),
        vmem((nt, nz, nt * chunk, units), BF16),
        vmem((nz, nt * chunk, quarter), BF16),
        vmem((nz, nt * chunk, quarter), BF16),
        vmem((nt * nrow, quarter), F32),
        vmem((nc, nx, group_rows, quarter), BF16),
        vmem((nx, group_rows, quarter), BF16),
        vmem((nx, group_rows, quarter), BF16),
        vmem((nx, group_rows, quarter), BF16),
        vmem((nt, rows, quarter), F32),
        vmem((nt, rows, quarter), F32),
        dma((13,)),
    ]
    for shape in (
        (2, nz // 2, 2),
        (2, nx),
        (2, nx),
        (2, nx),
        (nt,),
        (2, nt),
        (2, nt),
        (2, 2, nx),
        (nz,),
        (nz, nt),
        (nz, 2),
        (nz, nt),
        (nz // 2, 2),
        (nz,),
        (nx,),
        (nt,),
    ):
        scratch += [dma(shape), dma(shape)]
    in_vmem = pl.BlockSpec(memory_space=pltpu.VMEM)
    anywhere = pl.BlockSpec(memory_space=pl.ANY)
    out = pl.pallas_call(
        functools.partial(kernel, (nx, nz, nc, nt)),
        out_shape=jax.ShapeDtypeStruct((rows, width), BF16),
        in_specs=[pl.BlockSpec(memory_space=pltpu.SMEM)] + [anywhere] * 13,
        out_specs=in_vmem,
        scratch_shapes=scratch,
        compiler_params=pltpu.CompilerParams(
            collective_id=0, has_side_effects=True, vmem_limit_bytes=VMEM_LIMIT
        ),
        name="layer",
    )(
        lengths,
        new_keys[:, 0],
        new_values[:, 0],
        norm_gain.reshape(width // LANES, LANES),
        routes[0],
        route_weights[0],
        queries,
        cache_keys[:, 0],
        cache_values[:, 0],
        out_weight.T,
        residual[0],
        gate_weight[0],
        up_weight[0],
        down_weight[0],
    )
    return out[None]


def solution(mesh):
    placed = (
        P("ep", "tp", None),
        P("ep", "tp", None, None),
        P("ep", "tp", None, None),
        P("ep", "tp", None),
        P("ep", "tp", None),
        P("ep"),
        P("tp", "ep"),
        P("ep", "tp", None),
        P(),
        P("ep", "tp", None),
        P("ep", "tp", None),
        P("ep", None, "tp"),
        P("ep", None, "tp"),
        P("ep", "tp", None),
    )
    return jax.shard_map(
        functools.partial(on_device, mesh.shape["tp"]),
        mesh=mesh,
        in_specs=placed,
        out_specs=P("ep", "tp", None),
        check_vma=False,
    )
```

```python
import functools

import jax
import jax.numpy as jnp
from jax import lax
from jax.experimental import pallas as pl
from jax.experimental.pallas import tpu as pltpu
from jax.sharding import PartitionSpec as P

MESH = pl.DeviceIdType.MESH
BF16 = jnp.bfloat16
F32 = jnp.float32
EP_SHAPE = (4, 8, 2)
LANES = 128
CAP = 2
VMEM_LIMIT = 60 * 1024 * 1024


def dot(a, b):
    return jnp.dot(a, b, preferred_element_type=F32)


def dot_nt(a, b):
    return lax.dot_general(a, b, (((1,), (1,)), ((), ())), preferred_element_type=F32)


def offsets(nz):
    return {8: (-1, 2, -3, 4, 3, -2, 1, 0), 4: (-1, 2, 1, 0)}[nz]


def offset_of(index, nz):
    value = jnp.zeros_like(index)
    for i, d in enumerate(offsets(nz)):
        value = jnp.where(index == i, d, value)
    return value


def kernel(
    dims,
    lengths_ref,
    nk_hbm,
    nv_hbm,
    gain_hbm,
    routes_hbm,
    shares_hbm,
    q_hbm,
    k_hbm,
    v_hbm,
    wt_hbm,
    res_hbm,
    gate_hbm,
    up_hbm,
    down_hbm,
    out_ref,
    nk_ref,
    nv_ref,
    gain_ref,
    routes_ref,
    shares_ref,
    q_buf,
    k_buf,
    v_buf,
    mixed_buf,
    wg,
    xg,
    rs_send,
    rs_recv,
    projg,
    resg,
    hid,
    info,
    comb,
    sel,
    xs,
    gu,
    dwg,
    actg,
    ret_send,
    ret_recv,
    early_sum,
    fin_send,
    fin_pair,
    fin_sum,
    fin_recv,
    fy_send,
    fy_recv,
    load_sem,
    ring_ss,
    ring_rs,
    x_ss,
    x_rs,
    res_ss,
    res_rs,
    info_ss,
    info_rs,
    infoy_ss,
    infoy_rs,
    dw_ss,
    dw_rs,
    rs_ss,
    rs_rs,
    proj_ss,
    proj_rs,
    sel_ss,
    sel_rs,
    xs_ss,
    xs_rs,
    far_ss,
    far_rs,
    act_ss,
    act_rs,
    afar_ss,
    afar_rs,
    ret_ss,
    ret_rs,
    fin_ss,
    fin_rs,
    fy_ss,
    fy_rs,
):
    nx, nz, nc, nt = dims
    ns = nx * nc
    rows = res_hbm.shape[0]
    width = res_hbm.shape[1]
    quarter = width // nt
    group_rows = nt * rows
    heads, head_size = q_buf.shape[1], q_buf.shape[2]
    context = k_hbm.shape[1]
    hidden_units = gate_hbm.shape[1]
    chunk = ns * CAP

    ep = lax.axis_index("ep")
    t = lax.axis_index("tp")
    x = ep // (nz * nc)
    z = (ep // nc) % nz
    c = ep % nc
    s = x * nc + c

    def z_peer(d):
        return {"ep": (x * nz + (z + d + nz) % nz) * nc + c, "tp": t}

    sibling = {"ep": (x * nz + z) * nc + 1 - c, "tp": t}

    def x_index(d):
        return (x + d) % nx

    def x_peer(d):
        return {"ep": (x_index(d) * nz + z) * nc + c, "tp": t}

    def t_index(d):
        return (t + d) % nt

    def t_peer(d):
        return {"ep": ep, "tp": t_index(d)}

    pending = []

    def describe(src, dst, sems, at, peer):
        return pltpu.make_async_remote_copy(
            src_ref=src,
            dst_ref=dst,
            send_sem=sems[0].at[at],
            recv_sem=sems[1].at[at],
            device_id=peer,
            device_id_type=MESH,
        )

    def send(src, dst, sems, at, peer):
        copy = describe(src, dst, sems, at, peer)
        copy.start()
        pending.append(copy)

    def arrive(dst, sems, at):
        describe(dst, dst, sems, at, t_peer(1)).wait_recv()

    def spread_start(view, sems, own=None, pre=()):
        own = view(s) if own is None else own
        for d in range(1, nx):
            send(own, view(s), sems, pre + (0, d), x_peer(d))
        send(own, view(s), sems, pre + (1, 0), sibling)

    def spread_relay(view, sems, pre=()):
        for d in range(1, nx):
            block = view(x_index(nx - d) * nc + c)
            arrive(block, sems, pre + (0, d))
            send(block, block, sems, pre + (1, d), sibling)

    def spread_end(view, sems, pre=()):
        for d in range(nx):
            arrive(view(x_index(nx - d) * nc + 1 - c), sems, pre + (1, d))

    barrier = pltpu.get_barrier_semaphore()
    partners = (
        [z_peer(d) for d in range(1, nz)]
        + [x_peer(d) for d in range(1, nx)]
        + [sibling]
        + [t_peer(d) for d in range(1, nt)]
    )
    for peer in partners:
        pl.semaphore_signal(barrier, inc=1, device_id=peer, device_id_type=MESH)

    def load(src, dst, n):
        copy = pltpu.make_async_copy(src, dst, load_sem.at[n])
        copy.start()
        return copy

    q_load = load(q_hbm, q_buf, 0)
    k_load = load(k_hbm, k_buf.at[:, pl.ds(0, context)], 1)
    v_load = load(v_hbm, v_buf.at[:, pl.ds(0, context)], 2)
    small_loads = [
        load(src, dst, 8 + n)
        for n, (src, dst) in enumerate(
            (
                (nk_hbm, nk_ref),
                (nv_hbm, nv_ref),
                (gain_hbm, gain_ref),
                (routes_hbm, routes_ref),
                (shares_hbm, shares_ref),
            )
        )
    ]
    w_load = load(wt_hbm, wg.at[nz - 2], 3)
    r_load = load(res_hbm, resg.at[s], 4)

    lane = lax.broadcasted_iota(jnp.int32, (rows, LANES), 1)
    row = lax.broadcasted_iota(jnp.int32, (rows, LANES), 0)
    member = jnp.zeros((rows, LANES), F32)
    share = jnp.zeros((rows, LANES), F32)
    for n in (3, 4):
        small_loads[n].wait()
    routes = routes_ref[...]
    shares = shares_ref[...]
    for k in range(routes.shape[1]):
        hit = routes[:, k : k + 1] == lane
        member = jnp.where(hit, 1.0, member)
        share = share + jnp.where(hit, shares[:, k : k + 1], 0.0)
    rank = jnp.zeros((rows, LANES), F32)
    for j in range(rows - 1):
        rank = rank + jnp.where(row > j, member[j : j + 1, :], 0.0)
    info[t, s, 0] = jnp.where(member > 0.0, rank, -1.0)
    info[t, s, 1] = share

    pl.semaphore_wait(barrier, len(partners))

    half = nz // 2
    wrows = wt_hbm.shape[0]
    top, low = pl.ds(0, wrows // 2), pl.ds(wrows // 2, wrows // 2)

    pieces = (top, low)

    def ring_slot(side, j):
        return nz - 1 if j == half else 2 * (j - 1) + side

    def ring_send(j, k):
        for side, d in enumerate((1, -1)):
            if j == half and k != side:
                continue
            src = wt_hbm if j == 1 else wg.at[ring_slot(side, j - 1)]
            dst = wg.at[ring_slot(side, j), pieces[k]]
            send(src.at[pieces[k]], dst, (ring_ss, ring_rs), (side, j - 1, k), z_peer(d))

    def ring_wait(j, k):
        for side in range(2):
            if j == half and k != side:
                continue
            dst = wg.at[ring_slot(side, j), pieces[k]]
            arrive(dst, (ring_ss, ring_rs), (side, j - 1, k))

    events = [(j, k) for j in range(1, half) for k in range(2)]

    def ring_event():
        if events:
            j, k = events.pop(0)
            ring_wait(j, k)
            ring_send(j + 1, k)

    for k in range(2):
        ring_send(1, k)

    def info_of(p):
        return info.at[t, p]

    def res_of(p):
        return resg.at[p]

    def x_of(p):
        return xg.at[p]

    spread_start(info_of, (info_ss, info_rs))
    spread_start(res_of, (res_ss, res_rs), res_hbm)
    unit_cut = hidden_units * 3 // 4

    unit_parts = (pl.ds(0, unit_cut), pl.ds(unit_cut, hidden_units - unit_cut))

    def send_down(k):
        for d in range(1, nt):
            part = pl.ds(pl.multiple_of(t_index(d) * quarter, LANES), quarter)
            units = unit_parts[k]
            send(down_hbm.at[units, part], dwg.at[t, units], (dw_ss, dw_rs), (k, d), t_peer(d))

    send_down(0)

    tail = k_buf.shape[1] - context
    at_slot = lax.broadcasted_iota(jnp.int32, (group_rows, tail, head_size), 1) == 0
    for n in (0, 1, 2):
        small_loads[n].wait()
    for buf, fresh in ((k_buf, nk_ref), (v_buf, nv_ref)):
        value = jnp.where(at_slot, fresh[...].astype(F32)[:, None, :], 0.0)
        buf[:, context:, :] = value.astype(BF16)
    q_load.wait()
    k_load.wait()
    v_load.wait()
    g_load = load(gate_hbm, gu.at[:, pl.ds(0, hidden_units)], 5)
    u_load = load(up_hbm, gu.at[:, pl.ds(hidden_units, hidden_units)], 6)
    my_quarter = pl.ds(pl.multiple_of(t * quarter, LANES), quarter)
    d_load = load(down_hbm.at[:, my_quarter], dwg.at[t], 7)
    scale = head_size ** (-0.5)
    step_rows = 8

    def attend(g):
        slot = lax.broadcasted_iota(jnp.int32, (heads, context + tail), 1)
        rows_here = [g * step_rows + j for j in range(step_rows)]
        scores = [dot_nt(q_buf[r], k_buf[r]) for r in rows_here]
        probs = []
        for r, score in zip(rows_here, scores):
            valid = (slot < lengths_ref[r]) | (slot == context)
            score = jnp.where(valid, score * scale, -1e30)
            weight = jnp.exp(score - jnp.max(score, axis=1, keepdims=True))
            total = jnp.sum(weight, axis=1, keepdims=True)
            probs.append((weight * (1.0 / total)).astype(BF16))
        for r, prob in zip(rows_here, probs):
            mixed_buf[r] = dot(prob, v_buf[r])

    for g in range(group_rows // step_rows):
        attend(g)
        ring_event()
    for h in range(heads):
        xg[s, :, h * head_size : (h + 1) * head_size] = mixed_buf[:, h, :].astype(BF16)
    spread_start(x_of, (x_ss, x_rs))
    spread_relay(info_of, (info_ss, info_rs))
    spread_relay(res_of, (res_ss, res_rs))
    spread_end(info_of, (info_ss, info_rs))
    for d in range(1, nt):
        send(info.at[t], info.at[t], (infoy_ss, infoy_rs), (d,), t_peer(d))

    picks = nz * chunk
    slot_no = lax.broadcasted_iota(jnp.int32, (picks, LANES), 0)
    at_z = (z + offset_of(slot_no // chunk, nz) + nz) % nz
    expert = (x * nz + at_z) * nc + c
    spread = (lax.broadcasted_iota(jnp.int32, (picks, LANES), 1) == expert).astype(BF16)
    code = info[t, :, 0].reshape(ns * rows, LANES).astype(BF16)
    seen = dot_nt(spread, code)
    slot_no = lax.broadcasted_iota(jnp.int32, (picks, ns * rows), 0)
    row_no = lax.broadcasted_iota(jnp.int32, (picks, ns * rows), 1)
    pick = (
        (seen == (slot_no % CAP).astype(F32)) & (row_no // rows == (slot_no % chunk) // CAP)
    ).astype(BF16)

    while events:
        ring_event()
    spread_relay(x_of, (x_ss, x_rs))
    spread_end(x_of, (x_ss, x_rs))

    nrow = ns * rows
    ncol = half * wrows
    all_rows = xg[...].reshape(ns * group_rows, xg.shape[2])

    def project(q):
        cols = wg[q * half : (q + 1) * half].reshape(ncol, wg.shape[2])
        part = dot_nt(all_rows, cols).reshape(ns, nt, rows, ncol)
        for tt in range(nt):
            rs_send[q, tt] = part[:, tt].reshape(nrow, ncol).astype(BF16)
        for d in range(1, nt):
            send(rs_send.at[q, t_index(d)], rs_recv.at[q, t], (rs_ss, rs_rs), (q, d), t_peer(d))

    def proj_of(q):
        return lambda p: projg.at[q, p]

    def gather(q):
        total = rs_send[q, t].astype(F32)
        for d in range(1, nt):
            p = t_index(nt - d)
            arrive(rs_recv.at[q, p], (rs_ss, rs_rs), (q, d))
            total = total + rs_recv[q, p].astype(F32)
        projg[q, s] = total.astype(BF16)
        spread_start(proj_of(q), (proj_ss, proj_rs), pre=(q,))

    w_load.wait()
    project(0)
    ring_wait(half, 0)
    ring_wait(half, 1)
    project(1)
    gather(0)
    gather(1)
    send_down(1)
    spread_end(res_of, (res_ss, res_rs))
    r_load.wait()

    left_half = lax.broadcasted_iota(jnp.int32, (nrow, LANES), 1) < wrows
    squares = jnp.zeros((nrow, LANES), F32)
    npair = ncol // LANES
    for q in range(2):
        spread_relay(proj_of(q), (proj_ss, proj_rs), pre=(q,))
        spread_end(proj_of(q), (proj_ss, proj_rs), pre=(q,))
        for m in range(npair):
            j = q * npair + m + 1
            blocks = ((z - j + nz) % nz, (z + j) % nz) if j < half else (z, (z + half) % nz)
            lanes = slice(m * LANES, (m + 1) * LANES)
            for xx in range(nx):
                a = projg[q, xx * nc, :, lanes].astype(F32)
                b = projg[q, xx * nc + 1, :, lanes].astype(F32)
                pair = (
                    jnp.where(left_half, a, pltpu.roll(b, wrows, 1)),
                    jnp.where(left_half, pltpu.roll(a, wrows, 1), b),
                )
                for side in range(2):
                    col = pl.ds(pl.multiple_of((xx * nz + blocks[side]) * LANES, LANES), LANES)
                    base = resg[:, :, col].astype(F32).reshape(nrow, LANES)
                    value = base + pair[side]
                    hid[:, col] = value
                    squares = squares + value * value
    inverse = lax.rsqrt(jnp.sum(squares, axis=1, keepdims=True) * (1.0 / width) + 1e-06)
    cstep = min(width, 512)
    gain = gain_ref[...].astype(F32)
    for b in range(width // cstep):
        cs = slice(b * cstep, (b + 1) * cstep)
        values = []
        for j in range(b * cstep // LANES, (b + 1) * cstep // LANES):
            value = hid[:, j * LANES : (j + 1) * LANES] * inverse * gain[j : j + 1, :]
            values.append(value.astype(BF16))
        picked = dot(pick, jnp.concatenate(values, axis=1)).astype(BF16)
        xs[t, nz - 1, :, cs] = picked[(nz - 1) * chunk :]
        for i in range(nz - 1):
            sel[i, :, cs] = picked[i * chunk : (i + 1) * chunk]

    def send_chunk(i):
        if i < nz - 1:
            send(sel.at[i], xs.at[t, i], (sel_ss, sel_rs), (i,), z_peer(offsets(nz)[i]))

    for i in (0, 1):
        send_chunk(i)

    def forward(i):
        if i < nz - 1:
            arrive(xs.at[t, i], (sel_ss, sel_rs), (i,))
            send_chunk(i + 2)
        for d in (1, nt - 1):
            send(xs.at[t, i], xs.at[t, i], (xs_ss, xs_rs), (i, d), t_peer(d))

    def relay(i):
        for k, d in enumerate((1, nt - 1)):
            arrive(xs.at[t_index(nt - d), i], (xs_ss, xs_rs), (i, d))
            part = xs.at[t_index(nt - d), i, :, pl.ds(k * (width // 2), width // 2)]
            send(part, part, (far_ss, far_rs), (i, k), t_peer(d))

    def complete(i):
        for k in range(2):
            part = xs.at[t_index(nt // 2), i, :, pl.ds(k * (width // 2), width // 2)]
            arrive(part, (far_ss, far_rs), (i, k))

    per = 2
    groups = [range(k, k + per) for k in range(0, nz - per, per)]
    groups += [range(k, k + 1) for k in range(nz - per, nz)]

    forward(nz - 1)
    forward(0)
    relay(nz - 1)
    forward(1)
    relay(0)

    for d in range(1, nt):
        arrive(info.at[t_index(-d + nt)], (infoy_ss, infoy_rs), (d,))
    places = nz * nt * chunk
    block = nt * chunk
    slot_no = lax.broadcasted_iota(jnp.int32, (LANES, places), 1)
    at_z = (z + offset_of(slot_no // block, nz) + nz) % nz
    expert = (x * nz + at_z) * nc + c
    spread = (lax.broadcasted_iota(jnp.int32, (LANES, places), 0) == expert).astype(BF16)
    for tt in range(nt):
        code = info[tt, :, 0].reshape(nrow, LANES).astype(BF16)
        weight = info[tt, :, 1].reshape(nrow, LANES).astype(BF16)
        seen = dot(code, spread)
        given = dot(weight, spread)
        slot_no = lax.broadcasted_iota(jnp.int32, (nrow, places), 1)
        row_no = lax.broadcasted_iota(jnp.int32, (nrow, places), 0) + tt * nrow
        fits = (seen == (slot_no % CAP).astype(F32)) & (row_no // rows == (slot_no % block) // CAP)
        comb[tt * nrow : (tt + 1) * nrow, :] = jnp.where(fits, given, 0.0).astype(BF16)

    g_load.wait()
    u_load.wait()

    def first(p):
        chunks = groups[p]
        count = len(chunks)
        these = pl.ds(chunks[0], count)
        for i in chunks:
            complete(i)
        slots = xs[:, chunks[0] : chunks[-1] + 1].reshape(nt * count * chunk, width)
        both = dot(slots, gu[...])
        gate, up = both[:, :hidden_units], both[:, hidden_units:]
        act = (gate / (1.0 + jnp.exp(-gate)) * up).reshape(nt, count, chunk, hidden_units)
        for k in range(count):
            actg[t, chunks[k]] = act[:, k].reshape(block, hidden_units).astype(BF16)
        part = actg.at[t, these]
        for d in (1, nt - 1) if count > 1 else range(1, nt):
            send(part, part, (act_ss, act_rs), (p, d), t_peer(d))

    def relay_act(p):
        for k, d in enumerate((1, nt - 1)):
            src = t_index(nt - d)
            arrive(actg.at[src, pl.ds(groups[p][0], per)], (act_ss, act_rs), (p, d))
            part = actg.at[src, groups[p][k]]
            send(part, part, (afar_ss, afar_rs), (p, k), t_peer(d))

    def second(p):
        chunks = groups[p]
        count = len(chunks)
        if p == 0:
            d_load.wait()
            for d in range(1, nt):
                for k in range(2):
                    units = unit_parts[k]
                    arrive(dwg.at[t_index(-d + nt), units], (dw_ss, dw_rs), (k, d))
        if count > 1:
            for k in range(per):
                arrive(actg.at[t_index(nt // 2), chunks[k]], (afar_ss, afar_rs), (p, k))
        else:
            for d in range(1, nt):
                arrive(actg.at[t_index(nt - d), pl.ds(chunks[0], 1)], (act_ss, act_rs), (p, d))
        total = jnp.zeros((count * block, quarter), F32)
        for tt in range(nt):
            part = actg[tt, chunks[0] : chunks[-1] + 1].reshape(count * block, hidden_units)
            total = total + dot(part, dwg[tt])
        for k, i in enumerate(chunks):
            value = total[k * block : (k + 1) * block].astype(BF16)
            if i == nz - 1:
                ret_recv[i] = value
            else:
                ret_send[i] = value
                send(
                    ret_send.at[i],
                    ret_recv.at[i],
                    (ret_ss, ret_rs),
                    (i,),
                    z_peer(-offsets(nz)[i]),
                )

    last = len(groups) - 1
    relay(1)
    forward(2)
    first(0)
    for p in range(1, last + 1):
        for i in range(per * p, min(per * p + per, nz - 1)):
            if i + 1 < nz - 1:
                forward(i + 1)
            relay(i)
        if len(groups[p - 1]) > 1:
            relay_act(p - 1)
        first(p)
        second(p - 1)

    early = nz - per
    for i in range(early):
        arrive(ret_recv.at[i], (ret_ss, ret_rs), (i,))
    back = ret_recv[:early].reshape(early * block, quarter)
    early_sum[...] = dot(comb[:, : early * block], back)
    second(last)
    for i in range(early, nz - 1):
        arrive(ret_recv.at[i], (ret_ss, ret_rs), (i,))
    back = ret_recv[early:].reshape(per * block, quarter)
    for tt in range(nt):
        these = slice(tt * nrow, (tt + 1) * nrow)
        part = dot(comb[these, early * block :], back) + early_sum[these, :]
        part = part.reshape(nx, nc, rows, quarter).astype(BF16)
        for xx in range(nx):
            for cc in range(nc):
                fin_send[cc, xx, tt * rows : (tt + 1) * rows, :] = part[xx, cc]
    send(fin_send.at[1 - c], fin_pair, (fin_ss, fin_rs), (0,), sibling)
    arrive(fin_pair, (fin_ss, fin_rs), (0,))
    for d in sorted(range(1, nx), key=lambda d: -min(d, nx - d)):
        p = x_index(d)
        fin_sum[p] = (fin_send[c, p].astype(F32) + fin_pair[p].astype(F32)).astype(BF16)
        send(fin_sum.at[p], fin_recv.at[x], (fin_ss, fin_rs), (d,), x_peer(d))
    total = fin_send[c, x].astype(F32) + fin_pair[x].astype(F32)
    for d in range(1, nx):
        p = x_index(nx - d)
        arrive(fin_recv.at[p], (fin_ss, fin_rs), (d,))
        total = total + fin_recv[p].astype(F32)
    for tt in range(nt):
        fy_send[tt] = total[tt * rows : (tt + 1) * rows]
    for d in sorted(range(1, nt), key=lambda d: -min(d, nt - d)):
        send(fy_send.at[t_index(d)], fy_recv.at[t], (fy_ss, fy_rs), (d,), t_peer(d))
    fy_recv[t] = fy_send[t]
    for d in range(1, nt):
        arrive(fy_recv.at[t_index(-d + nt)], (fy_ss, fy_rs), (d,))
    own = pl.ds(pl.multiple_of(s * rows, rows), rows)
    for tt in range(nt):
        cs = slice(tt * quarter, (tt + 1) * quarter)
        out_ref[:, cs] = (hid[own, cs] + fy_recv[tt]).astype(BF16)
    for copy in pending:
        copy.wait_send()


def on_device(
    nt,
    queries,
    cache_keys,
    cache_values,
    new_keys,
    new_values,
    lengths,
    out_weight,
    residual,
    norm_gain,
    routes,
    route_weights,
    gate_weight,
    up_weight,
    down_weight,
):
    nx, nz, nc = EP_SHAPE
    ns = nx * nc
    group_rows, heads, head_size = queries.shape
    context = cache_keys.shape[2]
    flat = heads * head_size
    rows, width = residual.shape[1:]
    wcols = out_weight.shape[1]
    units = gate_weight.shape[2]
    quarter = width // nt
    chunk = ns * CAP
    nrow = ns * rows
    ncol = nz // 2 * wcols
    dma = pltpu.SemaphoreType.DMA
    vmem = pltpu.VMEM
    scratch = [
        vmem((group_rows, head_size), BF16),
        vmem((group_rows, head_size), BF16),
        vmem((width // LANES, LANES), BF16),
        vmem(routes.shape[1:], jnp.int32),
        vmem(routes.shape[1:], F32),
        vmem((group_rows, heads, head_size), BF16),
        vmem((group_rows, context + 16, head_size), BF16),
        vmem((group_rows, context + 16, head_size), BF16),
        vmem((group_rows, heads, head_size), F32),
        vmem((nz, wcols, flat), BF16),
        vmem((ns, group_rows, flat), BF16),
        vmem((2, nt, nrow, ncol), BF16),
        vmem((2, nt, nrow, ncol), BF16),
        vmem((2, ns, nrow, ncol), BF16),
        vmem((ns, rows, width), BF16),
        vmem((nrow, width), F32),
        vmem((nt, ns, 2, rows, LANES), F32),
        vmem((nt * nrow, nz * nt * chunk), BF16),
        vmem((nz, chunk, width), BF16),
        vmem((nt, nz, chunk, width), BF16),
        vmem((width, 2 * units), BF16),
        vmem((nt, units, quarter), BF16),
        vmem((nt, nz, nt * chunk, units), BF16),
        vmem((nz, nt * chunk, quarter), BF16),
        vmem((nz, nt * chunk, quarter), BF16),
        vmem((nt * nrow, quarter), F32),
        vmem((nc, nx, group_rows, quarter), BF16),
        vmem((nx, group_rows, quarter), BF16),
        vmem((nx, group_rows, quarter), BF16),
        vmem((nx, group_rows, quarter), BF16),
        vmem((nt, rows, quarter), F32),
        vmem((nt, rows, quarter), F32),
        dma((13,)),
    ]
    for shape in (
        (2, nz // 2, 2),
        (2, nx),
        (2, nx),
        (2, nx),
        (nt,),
        (2, nt),
        (2, nt),
        (2, 2, nx),
        (nz,),
        (nz, nt),
        (nz, 2),
        (nz, nt),
        (nz // 2, 2),
        (nz,),
        (nx,),
        (nt,),
    ):
        scratch += [dma(shape), dma(shape)]
    in_vmem = pl.BlockSpec(memory_space=pltpu.VMEM)
    anywhere = pl.BlockSpec(memory_space=pl.ANY)
    out = pl.pallas_call(
        functools.partial(kernel, (nx, nz, nc, nt)),
        out_shape=jax.ShapeDtypeStruct((rows, width), BF16),
        in_specs=[pl.BlockSpec(memory_space=pltpu.SMEM)] + [anywhere] * 13,
        out_specs=in_vmem,
        scratch_shapes=scratch,
        compiler_params=pltpu.CompilerParams(
            collective_id=0, has_side_effects=True, vmem_limit_bytes=VMEM_LIMIT
        ),
        name="layer",
    )(
        lengths,
        new_keys[:, 0],
        new_values[:, 0],
        norm_gain.reshape(width // LANES, LANES),
        routes[0],
        route_weights[0],
        queries,
        cache_keys[:, 0],
        cache_values[:, 0],
        out_weight.T,
        residual[0],
        gate_weight[0],
        up_weight[0],
        down_weight[0],
    )
    return out[None]


def solution(mesh):
    placed = (
        P("ep", "tp", None),
        P("ep", "tp", None, None),
        P("ep", "tp", None, None),
        P("ep", "tp", None),
        P("ep", "tp", None),
        P("ep"),
        P("tp", "ep"),
        P("ep", "tp", None),
        P(),
        P("ep", "tp", None),
        P("ep", "tp", None),
        P("ep", None, "tp"),
        P("ep", None, "tp"),
        P("ep", "tp", None),
    )
    return jax.shard_map(
        functools.partial(on_device, mesh.shape["tp"]),
        mesh=mesh,
        in_specs=placed,
        out_specs=P("ep", "tp", None),
        check_vma=False,
    )
```
